32 devices in a mesh: groups: 2 (over y), gx: 8 (over z, x), gy: 2 (over core).
Axes of the slice: x: 2, y: 2, z: 4, core: 2. Of those that a mesh axis runs over, the one named last changes fastest.
Arguments:
- voxels: bfloat16 [16, 128, 128, 64], P(('groups', 'gx'), 'gy'), parts along dimension 0, may hold values from -6 to 6
- occupancy: int32 [16, 128, 128], P(('groups', 'gx'), 'gy'), parts along dimension 0, may hold values 0 or 1
- row_weights: bfloat16 [8, 64], P('gx'), may hold values from -2 to 2
- column_weights: bfloat16 [128, 64], P('gy'), may hold values from -0.5 to 0.5
- depth_weights: bfloat16 [128, 64], replicated, may hold values from -0.5 to 0.5
- plane_kernels: bfloat16 [3, 2, 3, 3, 64, 64], replicated, may hold values from -0.25 to 0.25
- expand_weight: bfloat16 [64, 128], replicated, may hold values from -0.75 to 0.75
- shrink_weight: bfloat16 [128, 64], replicated, may hold values from -1 to 1
Outputs:
- updated: bfloat16 [16, 128, 128, 64], P(('groups', 'gx'), 'gy'), parts along dimension 0
The draws below stay inside these ranges and needn't reach their ends.
There are 2 independent parts, one for each index of `groups`. The reference program is written for one: setup_inputs(seed, part) draws one part's arguments, and reference() takes and returns one part's arrays. A program takes and returns all parts, laid end to end along the dimension named above; an argument that names none is the same for every part. Nothing has to cross between parts.
All inputs are finite; a program needn't handle non-finite values. No bound on the sum of `occupancy` on one device may be relied on, other than what follows from the above.
Results may differ from the reference program's by a relative error of at most 0.015.
Values may be sent and summed in bfloat16 or wider, within the bound.
No kernel may reach another device: no remote copies, remote signals or barrier semaphores. Data moves between devices by JAX's collectives and lax.ppermute only.
A program may use at most 64 MiB of HBM per device.

```python
import jax
import jax.numpy as jnp
from jax import lax

C = 64
H = 128
Z = 128
X = 8
Y = 128


def set_ends(result, own_key, smallest, largest):
    longest = result.shape.index(max(result.shape))
    spots = []
    for shift in (0, 1):
        where = [jax.random.randint(jax.random.fold_in(own_key, axis), (), 0, length) for axis, length in enumerate(result.shape)]
        where[longest] = (where[longest] + shift) % result.shape[longest]
        spots.append(tuple(where))
    return result.at[spots[0]].set(smallest).at[spots[1]].set(largest)


def levels(stream_key, extent, shards, low, high):
    level = 1.0
    for position, blocks in shards:
        draws = jax.random.uniform(jax.random.fold_in(jax.random.fold_in(stream_key, 6), position), (blocks,), jnp.float32, low / len(shards), high / len(shards))
        level = level * jnp.repeat(jnp.exp(draws), extent[position] // blocks).reshape((-1,) + (1,) * (len(extent) - 1 - position))
    return level


def centred(key, shape, spread, limit, cuts=(), dtype=jnp.bfloat16):
    entries = jax.random.normal(key, shape, jnp.float32) * spread
    if len(cuts) > 0:
        entries = levels(key, shape, cuts, -0.22, 0.18) * entries
    return jnp.clip(entries, min=-limit, max=limit).astype(dtype)


def setup_inputs(seed: int = 0, part: int = 0) -> dict:
    streams_of = jax.random.split(jax.random.key(seed), 9)
    part_keys = jax.random.split(jax.random.fold_in(streams_of[8], part), 9)
    voxels = centred(part_keys[0], (X, Y, Z, C), 1.0, 6.0, ((0, 8), (1, 2)))
    occupancy = set_ends((jax.random.randint(part_keys[1], (X, Y, Z), 0, 2) < 1).astype(jnp.int32), jax.random.fold_in(part_keys[1], 1), 0, 1)
    row_weights = centred(streams_of[2], (X, C), X ** -0.5, 2.0, ((0, 8),))
    column_weights = centred(streams_of[3], (Y, C), Y ** -0.5, 0.5, ((0, 2),))
    depth_weights = centred(streams_of[4], (Z, C), Z ** -0.5, 0.5)
    plane_kernels = centred(streams_of[5], (3, 2, 3, 3, C, C), (9 * C) ** -0.5, 0.25)
    expand_weight = centred(streams_of[6], (C, H), C ** -0.5, 0.75)
    shrink_weight = centred(streams_of[7], (H, C), (H // 4) ** -0.5, 1.0)
    return {"voxels": voxels, "occupancy": occupancy, "row_weights": row_weights, "column_weights": column_weights, "depth_weights": depth_weights, "plane_kernels": plane_kernels, "expand_weight": expand_weight, "shrink_weight": shrink_weight}


product_scale = 8.0


def conv_same(plane, kernel):
    rows = plane.shape[0]
    cols = plane.shape[1]
    padded = jnp.pad(plane.astype(jnp.float32), ((1, 1), (1, 1), (0, 0)))
    total = jnp.zeros((rows, cols, kernel.shape[-1]), jnp.float32)
    for row_off in range(3):
        for col_off in range(3):
            window = padded[row_off:row_off + rows, col_off:col_off + cols]
            total = total + jnp.einsum("ijc,co->ijo", window, kernel[row_off, col_off].astype(jnp.float32))
    return total


def plane_block(plane, kernels):
    inner = jax.nn.silu(conv_same(plane, kernels[0])).astype(jnp.bfloat16)
    return conv_same(inner, kernels[1]).astype(jnp.bfloat16)


def reference(voxels, occupancy, row_weights, column_weights, depth_weights, plane_kernels, expand_weight, shrink_weight):
    features = voxels * occupancy.astype(jnp.bfloat16)[..., None]
    widened = features.astype(jnp.float32)
    xy_plane = jnp.einsum("xyzc,zc->xyc", widened, depth_weights.astype(jnp.float32)).astype(jnp.bfloat16)
    xz_plane = jnp.einsum("xyzc,yc->xzc", widened, column_weights.astype(jnp.float32)).astype(jnp.bfloat16)
    yz_plane = jnp.einsum("xyzc,xc->yzc", widened, row_weights.astype(jnp.float32)).astype(jnp.bfloat16)
    xy_out = plane_block(xy_plane, plane_kernels[0])
    xz_out = plane_block(xz_plane, plane_kernels[1])
    yz_out = plane_block(yz_plane, plane_kernels[2])
    expand_wide = expand_weight.astype(jnp.float32)
    shrink_wide = shrink_weight.astype(jnp.float32)

    def per_slice(items):
        feature_slice, xy_row, xz_row = items
        product = xy_row.astype(jnp.float32)[:, None, :] * xz_row.astype(jnp.float32)[None, :, :]
        product = product * yz_out.astype(jnp.float32)
        mixed = (product_scale * product).astype(jnp.bfloat16).astype(jnp.float32)
        hidden = jax.nn.silu(jnp.einsum("yzc,ch->yzh", mixed, expand_wide)).astype(jnp.bfloat16)
        branch = jnp.einsum("yzh,hc->yzc", hidden.astype(jnp.float32), shrink_wide)
        return (feature_slice.astype(jnp.float32) + branch).astype(jnp.bfloat16)

    return lax.map(per_slice, (features, xy_out, xz_out))
```

```python
import functools

import jax
import jax.numpy as jnp
from jax import lax
from jax.experimental import pallas as pl
from jax.experimental.pallas import tpu as pltpu
from jax.sharding import PartitionSpec as P

product_scale = 8.0
f32 = jnp.float32
bf16 = jnp.bfloat16


def silu(v):
    half = 0.5 * v
    return half * jnp.tanh(half) + half


def taps(rows):
    n, c, w = rows.shape
    wide = rows.astype(f32).reshape(n * c, w)
    lane = lax.broadcasted_iota(jnp.int32, (n * c, w), 1)
    left = jnp.where(lane == 0, 0.0, pltpu.roll(wide, 1, 1)).astype(bf16).reshape(n, c, w)
    right = jnp.where(lane == w - 1, 0.0, pltpu.roll(wide, w - 1, 1)).astype(bf16).reshape(n, c, w)
    parts = [jnp.concatenate([left[i], rows[i], right[i]], axis=0) for i in range(n)]
    return jnp.concatenate(parts, axis=1)


def conv_rows(rows, weight):
    n, c, w = rows.shape
    full = jnp.dot(weight, taps(rows), preferred_element_type=f32)
    o = weight.shape[0] // 3
    out = []
    for i in range(n - 2):
        out.append(
            full[0:o, i * w : (i + 1) * w]
            + full[o : 2 * o, (i + 1) * w : (i + 2) * w]
            + full[2 * o : 3 * o, (i + 2) * w : (i + 3) * w]
        )
    return out


def small_kernel(valid_ref, near_ref, weight_ref, out_ref):
    for p in range(2):
        rows = jnp.stack([near_ref[i, p] for i in range(5)])
        inner = conv_rows(rows, weight_ref[p, 0])
        inner = jnp.stack([(silu(v) * valid_ref[i]).astype(bf16) for i, v in enumerate(inner)])
        out_ref[p] = conv_rows(inner, weight_ref[p, 1])[0].astype(bf16)


def main_kernel(
    ends_ref, plane_ref, vox_ref, occ_ref, small_ref, weight_ref, expand_ref, shrink_ref, out_ref, inner_ref, *, group
):
    rows, c, z = vox_ref.shape
    in_group = (rows + 2) // 3 if (rows + 2) % 3 == 0 else rows + 2
    for g in range((rows + 2) // in_group):
        base = g * in_group
        outs = conv_rows(plane_ref[base : base + in_group + 2], weight_ref[0])
        for i, v in enumerate(outs):
            v = silu(v)
            if base + i == 0:
                v = v * ends_ref[0]
            if base + i == rows + 1:
                v = v * ends_ref[1]
            inner_ref[base + i] = v.astype(bf16)
    xz = small_ref[1].astype(f32)
    xy = small_ref[0].astype(f32)
    for g in range(rows // group):
        base = g * group
        outs = conv_rows(inner_ref[base : base + group + 2], weight_ref[1])
        mixed = []
        for i, v in enumerate(outs):
            y = base + i
            product = xy[:, y : y + 1] * xz * v.astype(bf16).astype(f32)
            mixed.append((product_scale * product).astype(bf16))
        mixed = jnp.concatenate(mixed, axis=1)
        hidden = silu(jnp.dot(expand_ref[...], mixed, preferred_element_type=f32)).astype(bf16)
        branch = jnp.dot(shrink_ref[...], hidden, preferred_element_type=f32)
        for i in range(group):
            y = base + i
            feats = vox_ref[y].astype(f32) * occ_ref[y : y + 1].astype(f32)
            out_ref[y] = (feats + branch[:, i * z : (i + 1) * z]).astype(bf16)


def bit_of(axis, bit):
    return (lax.axis_index(axis) // bit) % 2 == 1


def swap(value, axis, bit):
    return lax.ppermute(value, axis, [(i, i ^ bit) for i in range(lax.axis_size(axis))])


def halve(total, axis, bit):
    half = total.shape[0] // 2
    upper = bit_of(axis, bit)
    low, high = total[:half], total[half:]
    sent = jnp.where(upper, low, high).astype(bf16)
    return jnp.where(upper, high, low).astype(f32) + swap(sent, axis, bit).astype(f32)


def whole(total, axis, bit):
    total = total.astype(bf16)
    return (total.astype(f32) + swap(total, axis, bit).astype(f32)).astype(bf16)


def join(part, axis, bit):
    other = swap(part, axis, bit)
    return jnp.where(
        bit_of(axis, bit), jnp.concatenate([other, part]), jnp.concatenate([part, other])
    )


def sum_lanes(lanes, axis):
    size = lax.axis_size(axis)
    bits = [1 << i for i in range(size.bit_length() - 1)]
    orders = [[bits[i % len(bits)]] + bits[: i % len(bits)] + bits[i % len(bits) + 1 :] for i in range(len(lanes))]
    done = [[] for _ in lanes]
    for step in range(len(bits)):
        for i, order in enumerate(orders):
            bit = order[step]
            if step < len(bits) - 1 and lanes[i].shape[0] % 2 == 0:
                lanes[i] = halve(lanes[i], axis, bit)
                done[i].append(bit)
            else:
                lanes[i] = whole(lanes[i], axis, bit)
    for step in range(max(len(d) for d in done)):
        for i, order in enumerate(done):
            if order:
                lanes[i] = join(lanes[i], axis, order.pop())
    return lanes


def shifted(value, axis, by):
    size = lax.axis_size(axis)
    pairs = [(i, i - by) for i in range(size) if 0 <= i - by < size]
    return lax.ppermute(value, axis, pairs)


def vmem():
    return pl.BlockSpec(memory_space=pltpu.VMEM)


def smem():
    return pl.BlockSpec(memory_space=pltpu.SMEM)


def stacked(kernel):
    a, b, c, o = kernel.shape
    return kernel.transpose(0, 3, 1, 2).reshape(a * o, b * c)


def shards(
    voxels, occupancy, row_weights, column_weights, depth_weights, plane_kernels, expand_weight, shrink_weight
):
    vox = voxels.transpose(0, 1, 3, 2)[0]
    occ = occupancy[0]
    rows, c, z = vox.shape
    features = vox.astype(f32) * occ.astype(f32)[:, None, :]
    gx, gy = lax.axis_index("gx"), lax.axis_index("gy")
    gx_size, gy_size = lax.axis_size("gx"), lax.axis_size("gy")

    part = features * row_weights[0].astype(f32)[None, :, None]
    lanes = sum_lanes([part[: rows // 2], part[rows // 2 :]], "gx")
    yz = jnp.concatenate([lane.astype(bf16) for lane in lanes])

    xy = jnp.sum(features * depth_weights.T.astype(f32)[None], axis=2).T.astype(bf16)
    xz_part = jnp.sum(features * column_weights.astype(f32)[:, :, None], axis=0)
    if gy_size == 2:
        other = swap(jnp.concatenate([xz_part, xy.astype(f32)], axis=1), "gy", 1)
        xz = xz_part + other[:, :z]
        other = other[:, z:].astype(bf16)
        xy = jnp.where(gy == 0, jnp.concatenate([xy, other], 1), jnp.concatenate([other, xy], 1))
    else:
        xz = lax.psum(xz_part, "gy")
        xy = lax.all_gather(xy, "gy", axis=1, tiled=True)
    planes = jnp.stack([xy, xz.astype(bf16)])
    near = jnp.stack([shifted(planes, "gx", by) if by else planes for by in (-2, -1, 0, 1, 2)])
    valid = jnp.stack([gx > 0, gx >= 0, gx < gx_size - 1]).astype(f32)
    weights = jnp.stack([jnp.stack([stacked(plane_kernels[p, l]) for l in range(2)]) for p in range(3)])
    small = pl.pallas_call(
        small_kernel,
        out_shape=jax.ShapeDtypeStruct(planes.shape, bf16),
        in_specs=[smem(), vmem(), vmem()],
        out_specs=vmem(),
        name="small",
    )(valid, near, weights[:2])
    small_xy = lax.dynamic_slice_in_dim(small[0], gy * rows, rows, 1)
    small = jnp.stack([jnp.pad(small_xy, ((0, 0), (0, z - rows))), small[1]])

    above = shifted(yz[rows - 2 :], "gy", -1)
    below = shifted(yz[:2], "gy", 1)
    plane = jnp.concatenate([above, yz, below])
    ends = jnp.stack([gy > 0, gy < gy_size - 1]).astype(f32)
    out = pl.pallas_call(
        functools.partial(main_kernel, group=16),
        out_shape=jax.ShapeDtypeStruct((rows, c, z), bf16),
        in_specs=[smem()] + [vmem()] * 7,
        out_specs=vmem(),
        scratch_shapes=[pltpu.VMEM((rows + 2, c, z), bf16)],
        compiler_params=pltpu.CompilerParams(vmem_limit_bytes=48 * 1024 * 1024),
        name="block",
    )(ends, plane, vox, occ, small, weights[2], expand_weight.T, shrink_weight.T)
    return out[None].transpose(0, 1, 3, 2)


def solution(mesh):
    in_specs = (
        P(("groups", "gx"), "gy", None, None),
        P(("groups", "gx"), "gy", None),
        P("gx", None),
        P("gy", None),
        P(),
        P(),
        P(),
        P(),
    )
    out_specs = P(("groups", "gx"), "gy", None, None)
    return jax.shard_map(shards, mesh=mesh, in_specs=in_specs, out_specs=out_specs, check_vma=False)
```

```python
import functools

import jax
import jax.numpy as jnp
from jax import lax
from jax.experimental import pallas as pl
from jax.experimental.pallas import tpu as pltpu
from jax.sharding import PartitionSpec as P

product_scale = 8.0
f32 = jnp.float32
bf16 = jnp.bfloat16


def with_halo(cells, sides, width):
    for axis, dim in sides:
        count = lax.axis_size(axis)
        ends = count - 1
        head = lax.slice_in_dim(cells, 0, width, axis=dim)
        tail = lax.slice_in_dim(cells, cells.shape[dim] - width, cells.shape[dim], axis=dim)
        cells = jnp.concatenate(
            [
                lax.ppermute(tail, axis, [(i, (i + 1) % count) for i in range(ends)]),
                cells,
                lax.ppermute(head, axis, [((i + 1) % count, i) for i in range(ends)]),
            ],
            axis=dim,
        )
    return cells


def conv_valid(padded, kernel):
    rows = padded.shape[0] - 2
    cols = padded.shape[1] - 2
    total = jnp.zeros((rows, cols, kernel.shape[-1]), jnp.float32)
    for row_off in range(3):
        for col_off in range(3):
            window = padded[row_off : row_off + rows, col_off : col_off + cols]
            total = total + jnp.einsum(
                "ijc,co->ijo", window, kernel[row_off, col_off], preferred_element_type=jnp.float32
            )
    return total


def plane_block(plane, kernels, extend):
    inner = jax.nn.silu(conv_valid(extend(plane), kernels[0])).astype(jnp.bfloat16)
    return conv_valid(extend(inner), kernels[1]).astype(jnp.bfloat16)


def rim_xy(plane):
    return with_halo(plane, (("gx", 0), ("gy", 1)), 1)


def rim_xz(plane):
    padded = with_halo(plane, (("gx", 0),), 1)
    return jnp.pad(padded, ((0, 0), (1, 1), (0, 0)))


def rim_yz(plane):
    padded = with_halo(plane, (("gy", 0),), 1)
    return jnp.pad(padded, ((0, 0), (1, 1), (0, 0)))


def general(
    voxels,
    occupancy,
    row_weights,
    column_weights,
    depth_weights,
    plane_kernels,
    expand_weight,
    shrink_weight,
):
    features = voxels * occupancy.astype(jnp.bfloat16)[..., None]
    xy_plane = jnp.einsum(
        "xyzc,zc->xyc", features, depth_weights, preferred_element_type=jnp.float32
    ).astype(jnp.bfloat16)
    xz_part = jnp.einsum(
        "xyzc,yc->xzc", features, column_weights, preferred_element_type=jnp.float32
    )
    yz_part = jnp.einsum("xyzc,xc->yzc", features, row_weights, preferred_element_type=jnp.float32)
    xy_out = plane_block(xy_plane, plane_kernels[0], rim_xy)
    xz_plane = lax.psum(xz_part, "gy").astype(jnp.bfloat16)
    xz_out = plane_block(xz_plane, plane_kernels[1], rim_xz)
    yz_plane = lax.psum(yz_part, "gx").astype(jnp.bfloat16)
    yz_out = plane_block(yz_plane, plane_kernels[2], rim_yz)
    product = xy_out.astype(jnp.float32)[:, :, None, :] * xz_out.astype(jnp.float32)[:, None, :, :]
    product = product * yz_out.astype(jnp.float32)[None, :, :, :]
    mixed = (product_scale * product).astype(jnp.bfloat16)
    hidden = jax.nn.silu(
        jnp.einsum("xyzc,ch->xyzh", mixed, expand_weight, preferred_element_type=jnp.float32)
    ).astype(jnp.bfloat16)
    branch = jnp.einsum("xyzh,hc->xyzc", hidden, shrink_weight, preferred_element_type=jnp.float32)
    return (features.astype(jnp.float32) + branch).astype(jnp.bfloat16)


def silu(v):
    half = 0.5 * v
    return half * jnp.tanh(half) + half


def taps(rows):
    n, c, w = rows.shape
    wide = rows.astype(f32).reshape(n * c, w)
    lane = lax.broadcasted_iota(jnp.int32, (n * c, w), 1)
    left = jnp.where(lane == 0, 0.0, pltpu.roll(wide, 1, 1)).astype(bf16).reshape(n, c, w)
    right = jnp.where(lane == w - 1, 0.0, pltpu.roll(wide, w - 1, 1)).astype(bf16).reshape(n, c, w)
    parts = [jnp.concatenate([left[i], rows[i], right[i]], axis=0) for i in range(n)]
    return jnp.concatenate(parts, axis=1)


def conv_rows(rows, weight):
    n, c, w = rows.shape
    full = jnp.dot(weight, taps(rows), preferred_element_type=f32)
    o = weight.shape[0] // 3
    out = []
    for i in range(n - 2):
        out.append(
            full[0:o, i * w : (i + 1) * w]
            + full[o : 2 * o, (i + 1) * w : (i + 2) * w]
            + full[2 * o : 3 * o, (i + 2) * w : (i + 3) * w]
        )
    return out


def place():
    return lax.axis_index("gx") % 4, lax.axis_index("gy")


def front_kernel(row_ref, vox_ref, occ_ref, *out_refs, chunk):
    rows, c, z = vox_ref.shape
    low, core = place()
    base = chunk_base(chunk, core, rows)
    quarter = rows // 8
    weight = row_ref[...].astype(f32)
    for d in (1, 2, 3, 0):
        first = base + jnp.bitwise_xor(low, d) * quarter
        occ = occ_ref[pl.ds(first, quarter)].astype(f32)
        for i in range(quarter):
            value = vox_ref[first + i].astype(f32) * occ[i : i + 1] * weight
            out_refs[d][i] = value.astype(out_refs[d].dtype)


def chunk_base(chunk, core, rows):
    half = rows // 2
    return (1 - core) * half if chunk == 0 else core * half


def sums_kernel(vox_ref, occ_ref, column_ref, depth_ref, after_ref, out_ref):
    del after_ref
    rows, c, z = vox_ref.shape
    depth = depth_ref[...].astype(f32)
    column = column_ref[...].astype(f32)
    lane = lax.broadcasted_iota(jnp.int32, (c, rows), 1)
    xz = jnp.zeros((c, z), f32)
    xy = jnp.zeros((c, rows), f32)
    for y in range(rows):
        feats = vox_ref[y].astype(f32) * occ_ref[y : y + 1].astype(f32)
        xz = xz + feats * column[:, y : y + 1]
        xy = jnp.where(lane == y, jnp.sum(feats * depth, axis=1, keepdims=True), xy)
    out_ref[:, :z] = xz
    out_ref[:, z:] = xy.astype(bf16).astype(f32)


def planes_kernel(own_ref, other_ref, after_ref, out_ref):
    del after_ref
    z = out_ref.shape[2]
    _, core = place()
    own, other = own_ref[...], other_ref[...]
    own_xy, other_xy = own[:, z:], other[:, z:]
    first = jnp.where(core == 0, own_xy, other_xy)
    second = jnp.where(core == 0, other_xy, own_xy)
    out_ref[0] = jnp.concatenate([first, second], axis=1).astype(bf16)
    out_ref[1] = (own[:, :z] + other[:, :z]).astype(bf16)


def weights_kernel(kernel_ref, after_ref, out_ref):
    del after_ref
    for p in range(kernel_ref.shape[0]):
        for l in range(kernel_ref.shape[1]):
            for a in range(3):
                rows = jnp.concatenate([kernel_ref[p, l, a, b] for b in range(3)], axis=0)
                o = rows.shape[1]
                out_ref[p, l, a * o : (a + 1) * o] = rows.astype(f32).T.astype(bf16)


def small_kernel(*refs, last):
    near_refs, weight_ref, after_ref, out_ref = refs[:5], refs[5], refs[6], refs[7]
    del after_ref
    at = lax.axis_index("gx")
    _, core = place()
    valid = [jnp.where(at > 0, 1.0, 0.0), 1.0, jnp.where(at < last, 1.0, 0.0)]
    for p in range(2):
        rows = jnp.stack([ref[p] for ref in near_refs])
        inner = conv_rows(rows, weight_ref[p, 0])
        inner = jnp.stack([(silu(v) * valid[i]).astype(bf16) for i, v in enumerate(inner)])
        value = conv_rows(inner, weight_ref[p, 1])[0]
        if p == 0:
            value = jnp.where(core == 0, value, pltpu.roll(value, value.shape[1] // 2, 1))
        out_ref[p] = value.astype(bf16)


def main_kernel(*refs, group):
    pieces, (halo_ref, vox_ref, occ_ref, small_ref, weight_ref, expand_ref, shrink_ref) = refs[:8], refs[8:15]
    out_ref, plane_ref, inner_ref = refs[15:]
    rows, c, z = vox_ref.shape
    low, core = place()
    quarter = rows // 8
    top = jnp.where(core == 0, 0.0, 1.0)
    bottom = 1.0 - top
    halo = halo_ref[...].astype(f32)
    plane_ref[0:2] = (halo * top).astype(bf16)
    plane_ref[rows + 2 : rows + 4] = (halo * bottom).astype(bf16)
    for chunk in range(2):
        for d in range(4):
            first = 2 + chunk_base(chunk, core, rows) + jnp.bitwise_xor(low, d) * quarter
            plane_ref[pl.ds(first, quarter)] = pieces[4 * chunk + d][...]
    in_group = (rows + 2) // 3 if (rows + 2) % 3 == 0 else rows + 2
    for g in range((rows + 2) // in_group):
        base = g * in_group
        outs = conv_rows(plane_ref[base : base + in_group + 2], weight_ref[0])
        for i, v in enumerate(outs):
            v = silu(v)
            if base + i == 0:
                v = v * top
            if base + i == rows + 1:
                v = v * bottom
            inner_ref[base + i] = v.astype(bf16)
    xz = small_ref[1].astype(f32)
    xy = small_ref[0].astype(f32)
    for g in range(rows // group):
        base = g * group
        outs = conv_rows(inner_ref[base : base + group + 2], weight_ref[1])
        mixed = []
        for i, v in enumerate(outs):
            y = base + i
            product = xy[:, y : y + 1] * xz * v.astype(bf16).astype(f32)
            mixed.append((product_scale * product).astype(bf16))
        mixed = jnp.concatenate(mixed, axis=1)
        hidden = silu(jnp.dot(expand_ref[...], mixed, preferred_element_type=f32)).astype(bf16)
        branch = jnp.dot(shrink_ref[...], hidden, preferred_element_type=f32)
        for i in range(group):
            y = base + i
            feats = vox_ref[y].astype(f32) * occ_ref[y : y + 1].astype(f32)
            out_ref[y] = (feats + branch[:, i * z : (i + 1) * z]).astype(bf16)


def swap(value, axis, bit):
    return lax.ppermute(value, axis, [(i, i ^ bit) for i in range(lax.axis_size(axis))])


def shifted(value, axis, by):
    size = lax.axis_size(axis)
    pairs = [(i, i - by) for i in range(size) if 0 <= i - by < size]
    return lax.ppermute(value, axis, pairs)


def vmem():
    return pl.BlockSpec(memory_space=pltpu.VMEM)


def anywhere():
    return pl.BlockSpec(memory_space=pl.ANY)


def call(kernel, name, out_shape, specs, scratch=()):
    return pl.pallas_call(
        kernel,
        out_shape=out_shape,
        in_specs=specs,
        out_specs=jax.tree.map(lambda _: vmem(), out_shape),
        scratch_shapes=list(scratch),
        compiler_params=pltpu.CompilerParams(vmem_limit_bytes=40 * 1024 * 1024),
        name=name,
    )


def shards(
    voxels, occupancy, row_weights, column_weights, depth_weights, plane_kernels, expand_weight, shrink_weight
):
    vox = voxels.transpose(0, 1, 3, 2)[0]
    occ = occupancy[0]
    rows, c, z = vox.shape
    low, core = place()
    quarter = rows // 8
    gx_size = lax.axis_size("gx")

    row_column = jnp.broadcast_to(row_weights[0][:, None], (c, z))
    piece = lambda kind: jax.ShapeDtypeStruct((quarter, c, z), kind)
    totals, arrived = [], []
    for chunk in range(2):
        own, *send = call(
            functools.partial(front_kernel, chunk=chunk), f"front{chunk}", [piece(f32)] + [piece(bf16)] * 3, [vmem()] * 3
        )(row_column, vox, occ)
        got = [swap(value, "gx", d) for d, value in zip((1, 2, 3), send)]
        arrived.append(got)
        totals.append((own + got[0].astype(f32) + got[1].astype(f32) + got[2].astype(f32)).astype(bf16))
    bit = 4
    while bit < gx_size:
        totals = [(t.astype(f32) + swap(t, "gx", bit).astype(f32)).astype(bf16) for t in totals]
        bit *= 2
    pieces = [[t] + [swap(t, "gx", d) for d in (1, 2, 3)] for t in totals]
    edge = jnp.bitwise_xor(low, jnp.where(core == 0, 3, 0))
    beside = pieces[0][0]
    for d in (1, 2, 3):
        beside = jnp.where(edge == d, pieces[0][d], beside)
    halo = swap(jnp.where(core == 0, beside[quarter - 2 :], beside[:2]), "gy", 1)

    message = call(
        sums_kernel, "sums", jax.ShapeDtypeStruct((c, z + rows), f32), [vmem()] * 4 + [anywhere()]
    )(vox, occ, column_weights.T, depth_weights.T, arrived[0][0])
    weights = call(
        weights_kernel,
        "weights",
        jax.ShapeDtypeStruct(plane_kernels.shape[:2] + (3 * c, 3 * c), bf16),
        [vmem(), anywhere()],
    )(plane_kernels, arrived[0][1])
    planes = call(
        planes_kernel, "planes", jax.ShapeDtypeStruct((2, c, z), bf16), [vmem()] * 2 + [anywhere()]
    )(message, swap(message, "gy", 1), totals[0])
    near = [shifted(planes, "gx", by) if by else planes for by in (-2, -1, 0, 1, 2)]
    small = call(
        functools.partial(small_kernel, last=gx_size - 1),
        "small",
        jax.ShapeDtypeStruct(planes.shape, bf16),
        [vmem()] * 6 + [anywhere()],
    )(*near, weights[:2], totals[1])

    out = call(
        functools.partial(main_kernel, group=16),
        "block",
        jax.ShapeDtypeStruct((rows, c, z), bf16),
        [vmem()] * 15,
        [pltpu.VMEM((rows + 4, c, z), bf16), pltpu.VMEM((rows + 2, c, z), bf16)],
    )(*pieces[0], *pieces[1], halo, vox, occ, small, weights[2], expand_weight.T, shrink_weight.T)
    return out[None].transpose(0, 1, 3, 2)


def solution(mesh):
    in_specs = (
        P(("groups", "gx"), "gy", None, None),
        P(("groups", "gx"), "gy", None),
        P("gx", None),
        P("gy", None),
        P(),
        P(),
        P(),
        P(),
    )
    out_specs = P(("groups", "gx"), "gy", None, None)

    def whole(voxels, *rest):
        gx, gy = mesh.shape["gx"], mesh.shape["gy"]
        x, y, z = voxels.shape[0] // mesh.shape["groups"], voxels.shape[1], voxels.shape[2]
        fits = gy == 2 and gx >= 4 and gx & (gx - 1) == 0 and x == gx and y == z and z == 128 and y % 32 == 0
        part = shards if fits else general
        mapped = jax.shard_map(part, mesh=mesh, in_specs=in_specs, out_specs=out_specs, check_vma=False)
        return mapped(voxels, *rest)

    return whole
```

```python
import functools

import jax
import jax.numpy as jnp
from jax import lax
from jax.experimental import pallas as pl
from jax.experimental.pallas import tpu as pltpu
from jax.sharding import PartitionSpec as P

product_scale = 8.0
f32 = jnp.float32
bf16 = jnp.bfloat16


def with_halo(cells, sides, width):
    for axis, dim in sides:
        count = lax.axis_size(axis)
        ends = count - 1
        head = lax.slice_in_dim(cells, 0, width, axis=dim)
        tail = lax.slice_in_dim(cells, cells.shape[dim] - width, cells.shape[dim], axis=dim)
        cells = jnp.concatenate(
            [
                lax.ppermute(tail, axis, [(i, (i + 1) % count) for i in range(ends)]),
                cells,
                lax.ppermute(head, axis, [((i + 1) % count, i) for i in range(ends)]),
            ],
            axis=dim,
        )
    return cells


def conv_valid(padded, kernel):
    rows = padded.shape[0] - 2
    cols = padded.shape[1] - 2
    total = jnp.zeros((rows, cols, kernel.shape[-1]), jnp.float32)
    for row_off in range(3):
        for col_off in range(3):
            window = padded[row_off : row_off + rows, col_off : col_off + cols]
            total = total + jnp.einsum(
                "ijc,co->ijo", window, kernel[row_off, col_off], preferred_element_type=jnp.float32
            )
    return total


def plane_block(plane, kernels, extend):
    inner = jax.nn.silu(conv_valid(extend(plane), kernels[0])).astype(jnp.bfloat16)
    return conv_valid(extend(inner), kernels[1]).astype(jnp.bfloat16)


def rim_xy(plane):
    return with_halo(plane, (("gx", 0), ("gy", 1)), 1)


def rim_xz(plane):
    padded = with_halo(plane, (("gx", 0),), 1)
    return jnp.pad(padded, ((0, 0), (1, 1), (0, 0)))


def rim_yz(plane):
    padded = with_halo(plane, (("gy", 0),), 1)
    return jnp.pad(padded, ((0, 0), (1, 1), (0, 0)))


def general(
    voxels,
    occupancy,
    row_weights,
    column_weights,
    depth_weights,
    plane_kernels,
    expand_weight,
    shrink_weight,
):
    features = voxels * occupancy.astype(jnp.bfloat16)[..., None]
    xy_plane = jnp.einsum(
        "xyzc,zc->xyc", features, depth_weights, preferred_element_type=jnp.float32
    ).astype(jnp.bfloat16)
    xz_part = jnp.einsum(
        "xyzc,yc->xzc", features, column_weights, preferred_element_type=jnp.float32
    )
    yz_part = jnp.einsum("xyzc,xc->yzc", features, row_weights, preferred_element_type=jnp.float32)
    xy_out = plane_block(xy_plane, plane_kernels[0], rim_xy)
    xz_plane = lax.psum(xz_part, "gy").astype(jnp.bfloat16)
    xz_out = plane_block(xz_plane, plane_kernels[1], rim_xz)
    yz_plane = lax.psum(yz_part, "gx").astype(jnp.bfloat16)
    yz_out = plane_block(yz_plane, plane_kernels[2], rim_yz)
    product = xy_out.astype(jnp.float32)[:, :, None, :] * xz_out.astype(jnp.float32)[:, None, :, :]
    product = product * yz_out.astype(jnp.float32)[None, :, :, :]
    mixed = (product_scale * product).astype(jnp.bfloat16)
    hidden = jax.nn.silu(
        jnp.einsum("xyzc,ch->xyzh", mixed, expand_weight, preferred_element_type=jnp.float32)
    ).astype(jnp.bfloat16)
    branch = jnp.einsum("xyzh,hc->xyzc", hidden, shrink_weight, preferred_element_type=jnp.float32)
    return (features.astype(jnp.float32) + branch).astype(jnp.bfloat16)


def silu(v):
    half = 0.5 * v
    return half * jnp.tanh(half) + half


def taps(rows):
    n, c, w = rows.shape
    wide = rows.astype(f32).reshape(n * c, w)
    lane = lax.broadcasted_iota(jnp.int32, (n * c, w), 1)
    left = jnp.where(lane == 0, 0.0, pltpu.roll(wide, 1, 1)).astype(bf16).reshape(n, c, w)
    right = jnp.where(lane == w - 1, 0.0, pltpu.roll(wide, w - 1, 1)).astype(bf16).reshape(n, c, w)
    parts = [jnp.concatenate([left[i], rows[i], right[i]], axis=0) for i in range(n)]
    return jnp.concatenate(parts, axis=1)


def conv_rows(rows, weight):
    n, c, w = rows.shape
    full = jnp.dot(weight, taps(rows), preferred_element_type=f32)
    o = weight.shape[0] // 3
    out = []
    for i in range(n - 2):
        out.append(
            full[0:o, i * w : (i + 1) * w]
            + full[o : 2 * o, (i + 1) * w : (i + 2) * w]
            + full[2 * o : 3 * o, (i + 2) * w : (i + 3) * w]
        )
    return out


def place():
    return lax.axis_index("gx") % 4, lax.axis_index("gy")


def weighted(vox, occ, row_ref, out_ref):
    weight = jnp.broadcast_to(row_ref[...].astype(f32), vox.shape[:0:-1]).T
    occ = occ.astype(f32)
    for i in range(vox.shape[0]):
        out_ref[i] = (vox[i].astype(f32) * occ[i : i + 1] * weight).astype(out_ref.dtype)


def quarter_at(rows, chunk, d):
    low, core = place()
    quarter = rows // 8
    return pl.multiple_of(chunk_base(chunk, core, rows) + jnp.bitwise_xor(low, d) * quarter, quarter)


def fetch_kernel(row_hbm, vox_hbm, occ_hbm, *refs):
    out_refs, (row_ref, vox_ref, occ_ref, row_sem, vox_sem, occ_sem) = refs[:4], refs[4:]
    rows = vox_hbm.shape[0]
    quarter = rows // 8
    copies = [pltpu.make_async_copy(row_hbm, row_ref, row_sem)]
    for d in (1, 2, 3, 0):
        part = pl.ds(quarter_at(rows, 0, d), quarter)
        copies.append(pltpu.make_async_copy(vox_hbm.at[part], vox_ref.at[d], vox_sem.at[d]))
        copies.append(pltpu.make_async_copy(occ_hbm.at[part], occ_ref.at[d], occ_sem.at[d]))
    for copy in copies:
        copy.start()
    for copy in copies:
        copy.wait()
    for d in (1, 2, 3, 0):
        weighted(vox_ref[d], occ_ref[d], row_ref, out_refs[d])


def front_kernel(row_ref, vox_ref, occ_ref, *out_refs):
    rows = vox_ref.shape[0]
    for d in (1, 2, 3, 0):
        part = pl.ds(quarter_at(rows, 1, d), rows // 8)
        weighted(vox_ref[part], occ_ref[part], row_ref, out_refs[d])


def chunk_base(chunk, core, rows):
    half = rows // 2
    return (1 - core) * half if chunk == 0 else core * half


def sums_kernel(vox_ref, occ_ref, column_ref, depth_ref, after_ref, out_ref):
    del after_ref
    rows, c, z = vox_ref.shape
    depth = depth_ref[...].astype(f32)
    columns = column_ref[...].astype(f32).T
    at = lax.broadcasted_iota(jnp.int32, (c, z), 1) % rows
    ones = jnp.ones((2 * z, z), bf16)
    xz = jnp.zeros((c, z), f32)
    xy = jnp.zeros((c, z), f32)
    group = 8
    for base in range(0, rows, group):
        terms = []
        for y in range(base, base + group):
            feats = vox_ref[y].astype(f32) * occ_ref[y : y + 1].astype(f32)
            xz = xz + feats * columns[:, y : y + 1]
            term = feats * depth
            high = term.astype(bf16)
            terms.append(jnp.concatenate([high, (term - high.astype(f32)).astype(bf16)], axis=1))
        total = jnp.dot(jnp.concatenate(terms, axis=0), ones, preferred_element_type=f32)
        for i in range(group):
            xy = jnp.where(at == base + i, total[i * c : (i + 1) * c], xy)
    out_ref[:, :z] = xz
    out_ref[:, z:] = xy.astype(bf16).astype(f32)


def merge_kernel(own_ref, first_ref, second_ref, third_ref, message_ref, other_ref, out_ref):
    quarter, c, z = own_ref.shape
    for i in range(quarter):
        total = own_ref[i] + first_ref[i].astype(f32) + second_ref[i].astype(f32) + third_ref[i].astype(f32)
        out_ref[i] = total.astype(bf16)
    _, core = place()
    lane = lax.broadcasted_iota(jnp.int32, (c, z), 1)
    here = (lane < z // 2) == (core == 0)
    out_ref[quarter] = jnp.where(here, message_ref[:, z:], other_ref[:, z:]).astype(bf16)
    out_ref[quarter + 1] = (message_ref[:, :z] + other_ref[:, :z]).astype(bf16)


def add_kernel(first_ref, second_ref, after_ref, out_ref):
    del after_ref
    out_ref[...] = (first_ref[...].astype(f32) + second_ref[...].astype(f32)).astype(bf16)


def join_kernel(sent_ref, got_ref, first_ref, second_ref, third_ref):
    quarter = sent_ref.shape[0] - 2
    for i in range(quarter):
        total = (sent_ref[i].astype(f32) + got_ref[i].astype(f32)).astype(bf16)
        for ref in (first_ref, second_ref, third_ref):
            ref[i] = total
    at = lax.axis_index("gx")
    odd = (at // 2 + at) % 2 == 1
    for p in range(2):
        own, far = sent_ref[quarter + p], got_ref[quarter + p]
        first_ref[quarter + p] = own
        second_ref[quarter + p] = own
        second_ref[quarter + 2 + p] = far
        third_ref[quarter + p] = jnp.where(odd, own.astype(f32), far.astype(f32)).astype(bf16)


def weights_kernel(kernel_ref, expand_ref, after_ref, small_ref, main_ref, expanded_ref):
    del after_ref
    expanded_ref[...] = expand_ref[...].astype(f32).T.astype(bf16)
    for p in range(kernel_ref.shape[0]):
        for l in range(kernel_ref.shape[1]):
            for a in range(3):
                rows = jnp.concatenate([kernel_ref[p, l, a, b] for b in range(3)], axis=0)
                o = rows.shape[1]
                value = rows.astype(f32).T.astype(bf16)
                if p < 2:
                    small_ref[p, l, a * o : (a + 1) * o] = value
                else:
                    main_ref[l, a * o : (a + 1) * o] = value


def small_kernel(*refs, last):
    near_refs, weight_ref, after_ref, out_ref = refs[:5], refs[5], refs[6], refs[7]
    del after_ref
    at = lax.axis_index("gx")
    _, core = place()
    valid = [jnp.where(at > 0, 1.0, 0.0), 1.0, jnp.where(at < last, 1.0, 0.0)]
    for p in range(2):
        rows = jnp.stack([ref[p] for ref in near_refs])
        inner = conv_rows(rows, weight_ref[p, 0])
        inner = jnp.stack([(silu(v) * valid[i]).astype(bf16) for i, v in enumerate(inner)])
        value = conv_rows(inner, weight_ref[p, 1])[0]
        if p == 0:
            value = jnp.where(core == 0, value, pltpu.roll(value, value.shape[1] // 2, 1))
        out_ref[p] = value.astype(bf16)


def block(rows_ref, inner_ref, masks, first, count, operands, stage_ref, out_hbm, sem):
    vox_ref, occ_ref, small_ref, weight_ref, expand_ref, shrink_ref = operands
    z = vox_ref.shape[2]
    inside = (count + 2) // 2
    for base in (0, inside):
        for i, v in enumerate(conv_rows(rows_ref[base : base + inside + 2], weight_ref[0])):
            v = silu(v)
            if base + i in masks:
                v = v * masks[base + i]
            inner_ref[base + i] = v.astype(bf16)
    xz = small_ref[1].astype(f32)
    xy = small_ref[0].astype(f32)
    start, other = first
    _, core = place()
    lanes = lambda by: pltpu.roll(xy, z - by, 1) if by else xy
    xy = jnp.where(core == 0, lanes(start), lanes(other))
    first = jnp.where(core == 0, start, other)
    group = count // 2
    copies = []
    for base in (0, group):
        mixed = []
        for i, v in enumerate(conv_rows(inner_ref[base : base + group + 2], weight_ref[1])):
            product = xy[:, base + i : base + i + 1] * xz * v.astype(bf16).astype(f32)
            mixed.append((product_scale * product).astype(bf16))
        mixed = jnp.concatenate(mixed, axis=1)
        hidden = silu(jnp.dot(expand_ref[...], mixed, preferred_element_type=f32)).astype(bf16)
        branch = jnp.dot(shrink_ref[...], hidden, preferred_element_type=f32)
        for i in range(group):
            y = first + base + i
            feats = vox_ref[y].astype(f32) * occ_ref[pl.ds(y, 1)].astype(f32)
            stage_ref[base + i] = (feats + branch[:, i * z : (i + 1) * z]).astype(bf16)
        part = pl.ds(base, group)
        copies.append(
            pltpu.make_async_copy(stage_ref.at[part], out_hbm.at[pl.ds(first + base, group)], sem.at[base // group])
        )
        copies[-1].start()
    for copy in copies:
        copy.wait()


def near_kernel(*refs):
    pieces, halo_ref, operands = refs[:4], refs[4], refs[5:11]
    out_hbm, edge_ref, rows_ref, inner_ref, stage_ref, sem = refs[11:]
    rows = operands[0].shape[0]
    quarter, half = rows // 8, rows // 2
    low, core = place()
    rows_ref[pl.ds(jnp.where(core == 0, half, 0), 2)] = halo_ref[...]
    for d in range(4):
        at = jnp.where(core == 0, 0, 2) + jnp.bitwise_xor(low, d) * quarter
        rows_ref[pl.ds(at, quarter)] = pieces[d][0:quarter]
    edge_ref[...] = rows_ref[pl.ds(jnp.where(core == 0, 0, half - 2), 4)]
    block(rows_ref, inner_ref, {}, (half + 2, 0), half - 2, operands, stage_ref, out_hbm, sem)


def rest_kernel(*refs):
    pieces, edge_ref, operands = refs[:4], refs[4], refs[5:11]
    _, out_hbm, rows_ref, inner_ref, stage_ref, sem = refs[11:]
    rows, c, z = operands[0].shape
    quarter, half = rows // 8, rows // 2
    low, core = place()
    rows_ref[pl.ds(jnp.where(core == 0, 0, half + 4), 2)] = jnp.zeros((2, c, z), bf16)
    rows_ref[pl.ds(jnp.where(core == 0, half + 2, 0), 4)] = edge_ref[...]
    for d in range(4):
        at = jnp.where(core == 0, 2, 4) + jnp.bitwise_xor(low, d) * quarter
        rows_ref[pl.ds(at, quarter)] = pieces[d][...]
    masks = {0: jnp.where(core == 0, 0.0, 1.0), half + 3: jnp.where(core == 0, 1.0, 0.0)}
    block(rows_ref, inner_ref, masks, (0, half - 2), half + 2, operands, stage_ref, out_hbm, sem)


def swap(value, axis, bit):
    return lax.ppermute(value, axis, [(i, i ^ bit) for i in range(lax.axis_size(axis))])


def shifted(value, axis, by):
    size = lax.axis_size(axis)
    pairs = [(i, i - by) for i in range(size) if 0 <= i - by < size]
    return lax.ppermute(value, axis, pairs)


def vmem():
    return pl.BlockSpec(memory_space=pltpu.VMEM)


def anywhere():
    return pl.BlockSpec(memory_space=pl.ANY)


def call(kernel, name, out_shape, specs, scratch=(), mib=40):
    return pl.pallas_call(
        kernel,
        out_shape=out_shape,
        in_specs=specs,
        out_specs=jax.tree.map(lambda _: vmem(), out_shape),
        scratch_shapes=list(scratch),
        compiler_params=pltpu.CompilerParams(vmem_limit_bytes=mib * 1024 * 1024),
        name=name,
    )


def shards(
    voxels, occupancy, row_weights, column_weights, depth_weights, plane_kernels, expand_weight, shrink_weight
):
    vox = voxels.transpose(0, 1, 3, 2)[0]
    occ = occupancy[0]
    rows, c, z = vox.shape
    low, core = place()
    quarter = rows // 8
    gx_size, gx = lax.axis_size("gx"), lax.axis_index("gx")

    piece = lambda kind, n=quarter: jax.ShapeDtypeStruct((n, c, z), kind)
    shapes = [piece(f32)] + [piece(bf16)] * 3
    scratch = [
        pltpu.VMEM(row_weights.shape, bf16),
        pltpu.VMEM((4, quarter, c, z), bf16),
        pltpu.VMEM((4, quarter, z), jnp.int32),
        pltpu.SemaphoreType.DMA,
        pltpu.SemaphoreType.DMA((4,)),
        pltpu.SemaphoreType.DMA((4,)),
    ]
    hbm = pl.BlockSpec(memory_space=pltpu.HBM)
    inputs = row_weights, vox, occ
    fronts = call(fetch_kernel, "fetch", shapes, [hbm] * 3, scratch, mib=62)(*inputs)
    fronts += call(front_kernel, "front", shapes, [vmem()] * 3)(*inputs)
    owns = [fronts[0], fronts[4]]
    gots = [[swap(fronts[4 * chunk + d], "gx", d) for d in (1, 2, 3)] for chunk in range(2)]

    message = call(
        sums_kernel, "sums", jax.ShapeDtypeStruct((c, 2 * z), f32), [vmem()] * 4 + [anywhere()]
    )(vox, occ, column_weights, depth_weights.T, gots[0][0])
    stacked = plane_kernels.shape[1:2] + (3 * c, 3 * c)
    small_weights, main_weights, expanded = call(
        weights_kernel,
        "weights",
        [
            jax.ShapeDtypeStruct((2,) + stacked, bf16),
            jax.ShapeDtypeStruct(stacked, bf16),
            jax.ShapeDtypeStruct(expand_weight.shape[::-1], bf16),
        ],
        [vmem()] * 2 + [anywhere()],
    )(plane_kernels, expand_weight, gots[1][0])
    merged = call(merge_kernel, "merge", piece(bf16, quarter + 2), [vmem()] * 6)(
        owns[0], *gots[0], message, swap(message, "gy", 1)
    )
    second = owns[1]
    for got in gots[1]:
        second = second + got.astype(f32)
    second = second.astype(bf16)
    add = lambda value, bit: (value.astype(f32) + swap(value, "gx", bit).astype(f32)).astype(bf16)
    planes = merged[quarter:]
    if gx_size == 8:
        sent = call(
            join_kernel, "join", [piece(bf16, quarter + n) for n in (2, 4, 2)], [vmem()] * 2
        )(merged, swap(merged, "gx", 4))
        got = [swap(value, "gx", d) for d, value in zip((1, 2, 3), sent)]
        second = call(add_kernel, "add", piece(bf16), [vmem()] * 2 + [anywhere()])(second, swap(second, "gx", 4), got[2])
        pieces = [[sent[0]] + got, None]
        one, two, three = (value[quarter:] for value in got)
        odd, right = gx // 2 % 2 == 1, gx % 2 == 1
        keep = lambda inside, value: jnp.where(inside, value, jnp.zeros_like(value))
        near = [
            keep(gx >= 2, jnp.where(odd, two[:2], two[2:])),
            keep(gx >= 1, jnp.where(right, one, three)),
            planes,
            keep(gx < gx_size - 1, jnp.where(right, three, one)),
            keep(gx < gx_size - 2, jnp.where(odd, two[2:], two[:2])),
        ]
    else:
        first, bit = merged[:quarter], 4
        while bit < gx_size:
            first, second = add(first, bit), add(second, bit)
            bit *= 2
        pieces = [[first] + [swap(first, "gx", d) for d in (1, 2, 3)], None]
        near = [shifted(planes, "gx", by) if by else planes for by in (-2, -1, 0, 1, 2)]
    pieces[1] = [second] + [swap(second, "gx", d) for d in (1, 2, 3)]
    edge = jnp.bitwise_xor(low, jnp.where(core == 0, 3, 0))
    beside = pieces[0][0][:quarter]
    for d in (1, 2, 3):
        beside = jnp.where(edge == d, pieces[0][d][:quarter], beside)
    halo = swap(jnp.where(core == 0, beside[quarter - 2 :], beside[:2]), "gy", 1)

    small = call(
        functools.partial(small_kernel, last=gx_size - 1),
        "small",
        jax.ShapeDtypeStruct(planes.shape, bf16),
        [vmem()] * 6 + [anywhere()],
    )(*near, small_weights, second)

    operands = vox, occ, small, main_weights, expanded, shrink_weight.T
    whole = jax.ShapeDtypeStruct((rows, c, z), bf16)
    half = rows // 2
    out, edge = pl.pallas_call(
        near_kernel,
        out_shape=[whole, piece(bf16, 4)],
        in_specs=[vmem()] * 11,
        out_specs=[hbm, vmem()],
        scratch_shapes=[pltpu.VMEM((n, c, z), bf16) for n in (half + 2, half, half - 2)] + [pltpu.SemaphoreType.DMA((2,))],
        compiler_params=pltpu.CompilerParams(vmem_limit_bytes=40 * 1024 * 1024),
        name="near",
    )(*pieces[0], halo, *operands)
    out = pl.pallas_call(
        rest_kernel,
        out_shape=whole,
        in_specs=[vmem()] * 11 + [hbm],
        out_specs=hbm,
        scratch_shapes=[pltpu.VMEM((n, c, z), bf16) for n in (half + 6, half + 4, half + 2)] + [pltpu.SemaphoreType.DMA((2,))],
        input_output_aliases={11: 0},
        compiler_params=pltpu.CompilerParams(vmem_limit_bytes=40 * 1024 * 1024),
        name="rest",
    )(*pieces[1], edge, *operands, out)
    return out[None].transpose(0, 1, 3, 2)


def solution(mesh):
    in_specs = (
        P(("groups", "gx"), "gy", None, None),
        P(("groups", "gx"), "gy", None),
        P("gx", None),
        P("gy", None),
        P(),
        P(),
        P(),
        P(),
    )
    out_specs = P(("groups", "gx"), "gy", None, None)

    def whole(voxels, *rest):
        gx, gy = mesh.shape["gx"], mesh.shape["gy"]
        x, y, z = voxels.shape[0] // mesh.shape["groups"], voxels.shape[1], voxels.shape[2]
        fits = gy == 2 and gx >= 4 and gx & (gx - 1) == 0 and x == gx and y == z and z == 128
        part = shards if fits else general
        mapped = jax.shard_map(part, mesh=mesh, in_specs=in_specs, out_specs=out_specs, check_vma=False)
        return mapped(voxels, *rest)

    return whole
```

```python
import functools

import jax
import jax.numpy as jnp
from jax import lax
from jax.experimental import pallas as pl
from jax.experimental.pallas import tpu as pltpu
from jax.sharding import PartitionSpec as P

product_scale = 8.0
f32 = jnp.float32
bf16 = jnp.bfloat16


def with_halo(cells, sides, width):
    for axis, dim in sides:
        count = lax.axis_size(axis)
        ends = count - 1
        head = lax.slice_in_dim(cells, 0, width, axis=dim)
        tail = lax.slice_in_dim(cells, cells.shape[dim] - width, cells.shape[dim], axis=dim)
        cells = jnp.concatenate(
            [
                lax.ppermute(tail, axis, [(i, (i + 1) % count) for i in range(ends)]),
                cells,
                lax.ppermute(head, axis, [((i + 1) % count, i) for i in range(ends)]),
            ],
            axis=dim,
        )
    return cells


def conv_valid(padded, kernel):
    rows = padded.shape[0] - 2
    cols = padded.shape[1] - 2
    total = jnp.zeros((rows, cols, kernel.shape[-1]), jnp.float32)
    for row_off in range(3):
        for col_off in range(3):
            window = padded[row_off : row_off + rows, col_off : col_off + cols]
            total = total + jnp.einsum(
                "ijc,co->ijo", window, kernel[row_off, col_off], preferred_element_type=jnp.float32
            )
    return total


def plane_block(plane, kernels, extend):
    inner = jax.nn.silu(conv_valid(extend(plane), kernels[0])).astype(jnp.bfloat16)
    return conv_valid(extend(inner), kernels[1]).astype(jnp.bfloat16)


def rim_xy(plane):
    return with_halo(plane, (("gx", 0), ("gy", 1)), 1)


def rim_xz(plane):
    padded = with_halo(plane, (("gx", 0),), 1)
    return jnp.pad(padded, ((0, 0), (1, 1), (0, 0)))


def rim_yz(plane):
    padded = with_halo(plane, (("gy", 0),), 1)
    return jnp.pad(padded, ((0, 0), (1, 1), (0, 0)))


def general(
    voxels,
    occupancy,
    row_weights,
    column_weights,
    depth_weights,
    plane_kernels,
    expand_weight,
    shrink_weight,
):
    features = voxels * occupancy.astype(jnp.bfloat16)[..., None]
    xy_plane = jnp.einsum(
        "xyzc,zc->xyc", features, depth_weights, preferred_element_type=jnp.float32
    ).astype(jnp.bfloat16)
    xz_part = jnp.einsum(
        "xyzc,yc->xzc", features, column_weights, preferred_element_type=jnp.float32
    )
    yz_part = jnp.einsum("xyzc,xc->yzc", features, row_weights, preferred_element_type=jnp.float32)
    xy_out = plane_block(xy_plane, plane_kernels[0], rim_xy)
    xz_plane = lax.psum(xz_part, "gy").astype(jnp.bfloat16)
    xz_out = plane_block(xz_plane, plane_kernels[1], rim_xz)
    yz_plane = lax.psum(yz_part, "gx").astype(jnp.bfloat16)
    yz_out = plane_block(yz_plane, plane_kernels[2], rim_yz)
    product = xy_out.astype(jnp.float32)[:, :, None, :] * xz_out.astype(jnp.float32)[:, None, :, :]
    product = product * yz_out.astype(jnp.float32)[None, :, :, :]
    mixed = (product_scale * product).astype(jnp.bfloat16)
    hidden = jax.nn.silu(
        jnp.einsum("xyzc,ch->xyzh", mixed, expand_weight, preferred_element_type=jnp.float32)
    ).astype(jnp.bfloat16)
    branch = jnp.einsum("xyzh,hc->xyzc", hidden, shrink_weight, preferred_element_type=jnp.float32)
    return (features.astype(jnp.float32) + branch).astype(jnp.bfloat16)


def silu(v):
    half = 0.5 * v
    return half * jnp.tanh(half) + half


def taps(rows):
    n, c, w = rows.shape
    wide = rows.astype(f32).reshape(n * c, w)
    lane = lax.broadcasted_iota(jnp.int32, (n * c, w), 1)
    left = jnp.where(lane == 0, 0.0, pltpu.roll(wide, 1, 1)).astype(bf16).reshape(n, c, w)
    right = jnp.where(lane == w - 1, 0.0, pltpu.roll(wide, w - 1, 1)).astype(bf16).reshape(n, c, w)
    parts = [jnp.concatenate([left[i], rows[i], right[i]], axis=0) for i in range(n)]
    return jnp.concatenate(parts, axis=1)


def conv_rows(rows, weight):
    n, c, w = rows.shape
    full = jnp.dot(weight, taps(rows), preferred_element_type=f32)
    o = weight.shape[0] // 3
    out = []
    for i in range(n - 2):
        out.append(
            full[0:o, i * w : (i + 1) * w]
            + full[o : 2 * o, (i + 1) * w : (i + 2) * w]
            + full[2 * o : 3 * o, (i + 2) * w : (i + 3) * w]
        )
    return out


def place():
    return lax.axis_index("gx") % 4, lax.axis_index("gy")


def weighted(vox, occ, row_ref, out_ref):
    weight = jnp.broadcast_to(row_ref[...].astype(f32), vox.shape[:0:-1]).T
    occ = occ.astype(f32)
    for i in range(vox.shape[0]):
        out_ref[i] = (vox[i].astype(f32) * occ[i : i + 1] * weight).astype(out_ref.dtype)


def quarter_at(rows, chunk, d):
    low, core = place()
    quarter = rows // 8
    return pl.multiple_of(chunk_base(chunk, core, rows) + jnp.bitwise_xor(low, d) * quarter, quarter)


def fetch_kernel(row_hbm, vox_hbm, occ_hbm, column_hbm, depth_hbm, *refs):
    out_refs, more_refs, (row_ref, vox_ref, occ_ref, row_sem, vox_sem, occ_sem, more_sem) = refs[:4], refs[4:6], refs[6:]
    rows = vox_hbm.shape[0]
    quarter = rows // 8
    copies = [pltpu.make_async_copy(row_hbm, row_ref, row_sem)]
    for d in (1, 2, 3, 0):
        part = pl.ds(quarter_at(rows, 0, d), quarter)
        copies.append(pltpu.make_async_copy(vox_hbm.at[part], vox_ref.at[d], vox_sem.at[d]))
        copies.append(pltpu.make_async_copy(occ_hbm.at[part], occ_ref.at[d], occ_sem.at[d]))
    for i, source in enumerate((column_hbm, depth_hbm)):
        copies.append(pltpu.make_async_copy(source, more_refs[i], more_sem.at[i]))
    for copy in copies:
        copy.start()
    for copy in copies:
        copy.wait()
    for d in (1, 2, 3, 0):
        weighted(vox_ref[d], occ_ref[d], row_ref, out_refs[d])


def front_kernel(row_ref, vox_ref, occ_ref, after_ref, *out_refs):
    del after_ref
    rows = vox_ref.shape[0]
    for d in (1, 2, 3, 0):
        part = pl.ds(quarter_at(rows, 1, d), rows // 8)
        weighted(vox_ref[part], occ_ref[part], row_ref, out_refs[d])


def chunk_base(chunk, core, rows):
    half = rows // 2
    return (1 - core) * half if chunk == 0 else core * half


def sums_kernel(vox_ref, occ_ref, column_ref, depth_ref, after_ref, out_ref):
    del after_ref
    rows, c, z = vox_ref.shape
    depth = depth_ref[...].astype(f32)
    columns = column_ref[...].astype(f32).T
    at = lax.broadcasted_iota(jnp.int32, (c, z), 1) % rows
    ones = jnp.ones((2 * z, z), bf16)
    xz = jnp.zeros((c, z), f32)
    xy = jnp.zeros((c, z), f32)
    group = 8
    for base in range(0, rows, group):
        terms = []
        for y in range(base, base + group):
            feats = vox_ref[y].astype(f32) * occ_ref[y : y + 1].astype(f32)
            xz = xz + feats * columns[:, y : y + 1]
            term = feats * depth
            high = term.astype(bf16)
            terms.append(jnp.concatenate([high, (term - high.astype(f32)).astype(bf16)], axis=1))
        total = jnp.dot(jnp.concatenate(terms, axis=0), ones, preferred_element_type=f32)
        for i in range(group):
            xy = jnp.where(at == base + i, total[i * c : (i + 1) * c], xy)
    out_ref[:, :z] = xz
    out_ref[:, z:] = xy.astype(bf16).astype(f32)


def merge_kernel(own_ref, first_ref, second_ref, third_ref, message_ref, other_ref, after_ref, out_ref):
    del after_ref
    quarter, c, z = own_ref.shape
    for i in range(quarter):
        total = own_ref[i] + first_ref[i].astype(f32) + second_ref[i].astype(f32) + third_ref[i].astype(f32)
        out_ref[i] = total.astype(bf16)
    _, core = place()
    lane = lax.broadcasted_iota(jnp.int32, (c, z), 1)
    here = (lane < z // 2) == (core == 0)
    out_ref[quarter] = jnp.where(here, message_ref[:, z:], other_ref[:, z:]).astype(bf16)
    out_ref[quarter + 1] = (message_ref[:, :z] + other_ref[:, :z]).astype(bf16)


def add_kernel(first_ref, second_ref, after_ref, out_ref):
    del after_ref
    out_ref[...] = (first_ref[...].astype(f32) + second_ref[...].astype(f32)).astype(bf16)


def join_kernel(sent_ref, got_ref, after_ref, first_ref, second_ref, third_ref):
    del after_ref
    quarter = sent_ref.shape[0] - 2
    for i in range(quarter):
        total = (sent_ref[i].astype(f32) + got_ref[i].astype(f32)).astype(bf16)
        for ref in (first_ref, second_ref, third_ref):
            ref[i] = total
    at = lax.axis_index("gx")
    odd = (at // 2 + at) % 2 == 1
    for p in range(2):
        own, far = sent_ref[quarter + p], got_ref[quarter + p]
        first_ref[quarter + p] = own
        second_ref[quarter + p] = own
        second_ref[quarter + 2 + p] = far
        third_ref[quarter + p] = jnp.where(odd, own.astype(f32), far.astype(f32)).astype(bf16)


def weights_kernel(kernel_ref, expand_ref, after_ref, small_ref, main_ref, expanded_ref):
    del after_ref
    expanded_ref[...] = expand_ref[...].astype(f32).T.astype(bf16)
    for p in range(kernel_ref.shape[0]):
        for l in range(kernel_ref.shape[1]):
            for a in range(3):
                rows = jnp.concatenate([kernel_ref[p, l, a, b] for b in range(3)], axis=0)
                o = rows.shape[1]
                value = rows.astype(f32).T.astype(bf16)
                if p < 2:
                    small_ref[p, l, a * o : (a + 1) * o] = value
                else:
                    main_ref[l, a * o : (a + 1) * o] = value


def small_kernel(*refs, last):
    near_refs, weight_ref, after_ref, out_ref = refs[:5], refs[5], refs[6], refs[7]
    del after_ref
    at = lax.axis_index("gx")
    _, core = place()
    valid = [jnp.where(at > 0, 1.0, 0.0), 1.0, jnp.where(at < last, 1.0, 0.0)]
    for p in range(2):
        rows = jnp.stack([ref[p] for ref in near_refs])
        inner = conv_rows(rows, weight_ref[p, 0])
        inner = jnp.stack([(silu(v) * valid[i]).astype(bf16) for i, v in enumerate(inner)])
        value = conv_rows(inner, weight_ref[p, 1])[0]
        if p == 0:
            value = jnp.where(core == 0, value, pltpu.roll(value, value.shape[1] // 2, 1))
        out_ref[p] = value.astype(bf16)


def block(rows_ref, inner_ref, masks, first, count, operands, stage_ref, out_hbm, sem):
    vox_ref, occ_ref, small_ref, weight_ref, expand_ref, shrink_ref = operands
    z = vox_ref.shape[2]
    inside = (count + 2) // 2
    for base in (0, inside):
        for i, v in enumerate(conv_rows(rows_ref[base : base + inside + 2], weight_ref[0])):
            v = silu(v)
            if base + i in masks:
                v = v * masks[base + i]
            inner_ref[base + i] = v.astype(bf16)
    xz = small_ref[1].astype(f32)
    xy = small_ref[0].astype(f32)
    start, other = first
    _, core = place()
    lanes = lambda by: pltpu.roll(xy, z - by, 1) if by else xy
    xy = jnp.where(core == 0, lanes(start), lanes(other))
    first = jnp.where(core == 0, start, other)
    group = count // 2
    copies = []
    for base in (0, group):
        mixed = []
        for i, v in enumerate(conv_rows(inner_ref[base : base + group + 2], weight_ref[1])):
            product = xy[:, base + i : base + i + 1] * xz * v.astype(bf16).astype(f32)
            mixed.append((product_scale * product).astype(bf16))
        mixed = jnp.concatenate(mixed, axis=1)
        hidden = silu(jnp.dot(expand_ref[...], mixed, preferred_element_type=f32)).astype(bf16)
        branch = jnp.dot(shrink_ref[...], hidden, preferred_element_type=f32)
        for i in range(group):
            y = first + base + i
            feats = vox_ref[y].astype(f32) * occ_ref[pl.ds(y, 1)].astype(f32)
            stage_ref[base + i] = (feats + branch[:, i * z : (i + 1) * z]).astype(bf16)
        part = pl.ds(base, group)
        copies.append(
            pltpu.make_async_copy(stage_ref.at[part], out_hbm.at[pl.ds(first + base, group)], sem.at[base // group])
        )
        copies[-1].start()
    for copy in copies:
        copy.wait()


def near_kernel(*refs):
    pieces, halo_ref, operands = refs[:4], refs[4], refs[5:11]
    out_hbm, edge_ref, rows_ref, inner_ref, stage_ref, sem = refs[11:]
    rows = operands[0].shape[0]
    quarter, half = rows // 8, rows // 2
    low, core = place()
    rows_ref[pl.ds(jnp.where(core == 0, half, 0), 2)] = halo_ref[...]
    for d in range(4):
        at = jnp.where(core == 0, 0, 2) + jnp.bitwise_xor(low, d) * quarter
        rows_ref[pl.ds(at, quarter)] = pieces[d][0:quarter]
    edge_ref[...] = rows_ref[pl.ds(jnp.where(core == 0, 0, half - 2), 4)]
    block(rows_ref, inner_ref, {}, (half + 2, 0), half - 2, operands, stage_ref, out_hbm, sem)


def rest_kernel(*refs):
    pieces, edge_ref, operands = refs[:4], refs[4], refs[5:11]
    _, out_hbm, rows_ref, inner_ref, stage_ref, sem = refs[11:]
    rows, c, z = operands[0].shape
    quarter, half = rows // 8, rows // 2
    low, core = place()
    rows_ref[pl.ds(jnp.where(core == 0, 0, half + 4), 2)] = jnp.zeros((2, c, z), bf16)
    rows_ref[pl.ds(jnp.where(core == 0, half + 2, 0), 4)] = edge_ref[...]
    for d in range(4):
        at = jnp.where(core == 0, 2, 4) + jnp.bitwise_xor(low, d) * quarter
        rows_ref[pl.ds(at, quarter)] = pieces[d][...]
    masks = {0: jnp.where(core == 0, 0.0, 1.0), half + 3: jnp.where(core == 0, 1.0, 0.0)}
    block(rows_ref, inner_ref, masks, (0, half - 2), half + 2, operands, stage_ref, out_hbm, sem)


def swap(value, axis, bit):
    return lax.ppermute(value, axis, [(i, i ^ bit) for i in range(lax.axis_size(axis))])


def shifted(value, axis, by):
    size = lax.axis_size(axis)
    pairs = [(i, i - by) for i in range(size) if 0 <= i - by < size]
    return lax.ppermute(value, axis, pairs)


def vmem():
    return pl.BlockSpec(memory_space=pltpu.VMEM)


def anywhere():
    return pl.BlockSpec(memory_space=pl.ANY)


def call(kernel, name, out_shape, specs, scratch=(), mib=40):
    return pl.pallas_call(
        kernel,
        out_shape=out_shape,
        in_specs=specs,
        out_specs=jax.tree.map(lambda _: vmem(), out_shape),
        scratch_shapes=list(scratch),
        compiler_params=pltpu.CompilerParams(vmem_limit_bytes=mib * 1024 * 1024),
        name=name,
    )


def shards(
    voxels, occupancy, row_weights, column_weights, depth_weights, plane_kernels, expand_weight, shrink_weight
):
    vox = voxels.transpose(0, 1, 3, 2)[0]
    occ = occupancy[0]
    rows, c, z = vox.shape
    low, core = place()
    quarter = rows // 8
    gx_size, gx = lax.axis_size("gx"), lax.axis_index("gx")

    piece = lambda kind, n=quarter: jax.ShapeDtypeStruct((n, c, z), kind)
    shapes = [piece(f32)] + [piece(bf16)] * 3
    scratch = [
        pltpu.VMEM(row_weights.shape, bf16),
        pltpu.VMEM((4, quarter, c, z), bf16),
        pltpu.VMEM((4, quarter, z), jnp.int32),
        pltpu.SemaphoreType.DMA,
        pltpu.SemaphoreType.DMA((4,)),
        pltpu.SemaphoreType.DMA((4,)),
        pltpu.SemaphoreType.DMA((2,)),
    ]
    hbm = pl.BlockSpec(memory_space=pltpu.HBM)
    more = column_weights, depth_weights.T
    more_shapes = [jax.ShapeDtypeStruct(value.shape, bf16) for value in more]
    *first, column, depth = call(fetch_kernel, "fetch", shapes + more_shapes, [hbm] * 5, scratch, mib=62)(
        row_weights, vox, occ, *more
    )
    partners = lambda values: [swap(value, "gx", d) for d, value in zip((1, 2, 3), values)]
    first_got = partners(first[1:])
    stacked = plane_kernels.shape[1:2] + (3 * c, 3 * c)
    small_weights, main_weights, expanded = call(
        weights_kernel,
        "weights",
        [
            jax.ShapeDtypeStruct((2,) + stacked, bf16),
            jax.ShapeDtypeStruct(stacked, bf16),
            jax.ShapeDtypeStruct(expand_weight.shape[::-1], bf16),
        ],
        [vmem()] * 2 + [anywhere()],
    )(plane_kernels, expand_weight, first_got[0])
    message = call(
        sums_kernel, "sums", jax.ShapeDtypeStruct((c, 2 * z), f32), [vmem()] * 4 + [anywhere()]
    )(vox, occ, column, depth, expanded)
    own, *send = call(front_kernel, "front", shapes, [vmem()] * 3 + [anywhere()])(row_weights, vox, occ, message)
    owns, gots = [first[0], own], [first_got, partners(send)]

    merged = call(merge_kernel, "merge", piece(bf16, quarter + 2), [vmem()] * 6 + [anywhere()])(
        owns[0], *gots[0], message, swap(message, "gy", 1), owns[1]
    )
    second = owns[1]
    for got in gots[1]:
        second = second + got.astype(f32)
    second = second.astype(bf16)
    add = lambda value, bit: (value.astype(f32) + swap(value, "gx", bit).astype(f32)).astype(bf16)
    planes = merged[quarter:]
    if gx_size == 8:
        sent = call(
            join_kernel, "join", [piece(bf16, quarter + n) for n in (2, 4, 2)], [vmem()] * 2 + [anywhere()]
        )(merged, swap(merged, "gx", 4), gots[1][2])
        got = [swap(value, "gx", d) for d, value in zip((1, 2, 3), sent)]
        second = call(add_kernel, "add", piece(bf16), [vmem()] * 2 + [anywhere()])(second, swap(second, "gx", 4), got[2])
        pieces = [[sent[0]] + got, None]
        one, two, three = (value[quarter:] for value in got)
        odd, right = gx // 2 % 2 == 1, gx % 2 == 1
        keep = lambda inside, value: jnp.where(inside, value, jnp.zeros_like(value))
        near = [
            keep(gx >= 2, jnp.where(odd, two[:2], two[2:])),
            keep(gx >= 1, jnp.where(right, one, three)),
            planes,
            keep(gx < gx_size - 1, jnp.where(right, three, one)),
            keep(gx < gx_size - 2, jnp.where(odd, two[2:], two[:2])),
        ]
    else:
        first, bit = merged[:quarter], 4
        while bit < gx_size:
            first, second = add(first, bit), add(second, bit)
            bit *= 2
        pieces = [[first] + [swap(first, "gx", d) for d in (1, 2, 3)], None]
        near = [shifted(planes, "gx", by) if by else planes for by in (-2, -1, 0, 1, 2)]
    pieces[1] = [second] + [swap(second, "gx", d) for d in (1, 2, 3)]
    edge = jnp.bitwise_xor(low, jnp.where(core == 0, 3, 0))
    beside = pieces[0][0][:quarter]
    for d in (1, 2, 3):
        beside = jnp.where(edge == d, pieces[0][d][:quarter], beside)
    halo = swap(jnp.where(core == 0, beside[quarter - 2 :], beside[:2]), "gy", 1)

    small = call(
        functools.partial(small_kernel, last=gx_size - 1),
        "small",
        jax.ShapeDtypeStruct(planes.shape, bf16),
        [vmem()] * 6 + [anywhere()],
    )(*near, small_weights, second)

    operands = vox, occ, small, main_weights, expanded, shrink_weight.T
    whole = jax.ShapeDtypeStruct((rows, c, z), bf16)
    half = rows // 2
    out, edge = pl.pallas_call(
        near_kernel,
        out_shape=[whole, piece(bf16, 4)],
        in_specs=[vmem()] * 11,
        out_specs=[hbm, vmem()],
        scratch_shapes=[pltpu.VMEM((n, c, z), bf16) for n in (half + 2, half, half - 2)] + [pltpu.SemaphoreType.DMA((2,))],
        compiler_params=pltpu.CompilerParams(vmem_limit_bytes=40 * 1024 * 1024),
        name="near",
    )(*pieces[0], halo, *operands)
    out = pl.pallas_call(
        rest_kernel,
        out_shape=whole,
        in_specs=[vmem()] * 11 + [hbm],
        out_specs=hbm,
        scratch_shapes=[pltpu.VMEM((n, c, z), bf16) for n in (half + 6, half + 4, half + 2)] + [pltpu.SemaphoreType.DMA((2,))],
        input_output_aliases={11: 0},
        compiler_params=pltpu.CompilerParams(vmem_limit_bytes=40 * 1024 * 1024),
        name="rest",
    )(*pieces[1], edge, *operands, out)
    return out[None].transpose(0, 1, 3, 2)


def solution(mesh):
    in_specs = (
        P(("groups", "gx"), "gy", None, None),
        P(("groups", "gx"), "gy", None),
        P("gx", None),
        P("gy", None),
        P(),
        P(),
        P(),
        P(),
    )
    out_specs = P(("groups", "gx"), "gy", None, None)

    def whole(voxels, *rest):
        gx, gy = mesh.shape["gx"], mesh.shape["gy"]
        x, y, z = voxels.shape[0] // mesh.shape["groups"], voxels.shape[1], voxels.shape[2]
        fits = gy == 2 and gx >= 4 and gx & (gx - 1) == 0 and x == gx and y == z and z == 128
        part = shards if fits else general
        mapped = jax.shard_map(part, mesh=mesh, in_specs=in_specs, out_specs=out_specs, check_vma=False)
        return mapped(voxels, *rest)

    return whole
```

```python
import functools

import jax
import jax.numpy as jnp
from jax import lax
from jax.experimental import pallas as pl
from jax.experimental.pallas import tpu as pltpu
from jax.sharding import PartitionSpec as P

product_scale = 8.0
f32 = jnp.float32
bf16 = jnp.bfloat16


def with_halo(cells, sides, width):
    for axis, dim in sides:
        count = lax.axis_size(axis)
        ends = count - 1
        head = lax.slice_in_dim(cells, 0, width, axis=dim)
        tail = lax.slice_in_dim(cells, cells.shape[dim] - width, cells.shape[dim], axis=dim)
        cells = jnp.concatenate(
            [
                lax.ppermute(tail, axis, [(i, (i + 1) % count) for i in range(ends)]),
                cells,
                lax.ppermute(head, axis, [((i + 1) % count, i) for i in range(ends)]),
            ],
            axis=dim,
        )
    return cells


def conv_valid(padded, kernel):
    rows = padded.shape[0] - 2
    cols = padded.shape[1] - 2
    total = jnp.zeros((rows, cols, kernel.shape[-1]), jnp.float32)
    for row_off in range(3):
        for col_off in range(3):
            window = padded[row_off : row_off + rows, col_off : col_off + cols]
            total = total + jnp.einsum(
                "ijc,co->ijo", window, kernel[row_off, col_off], preferred_element_type=jnp.float32
            )
    return total


def plane_block(plane, kernels, extend):
    inner = jax.nn.silu(conv_valid(extend(plane), kernels[0])).astype(jnp.bfloat16)
    return conv_valid(extend(inner), kernels[1]).astype(jnp.bfloat16)


def rim_xy(plane):
    return with_halo(plane, (("gx", 0), ("gy", 1)), 1)


def rim_xz(plane):
    padded = with_halo(plane, (("gx", 0),), 1)
    return jnp.pad(padded, ((0, 0), (1, 1), (0, 0)))


def rim_yz(plane):
    padded = with_halo(plane, (("gy", 0),), 1)
    return jnp.pad(padded, ((0, 0), (1, 1), (0, 0)))


def general(
    voxels,
    occupancy,
    row_weights,
    column_weights,
    depth_weights,
    plane_kernels,
    expand_weight,
    shrink_weight,
):
    features = voxels * occupancy.astype(jnp.bfloat16)[..., None]
    xy_plane = jnp.einsum(
        "xyzc,zc->xyc", features, depth_weights, preferred_element_type=jnp.float32
    ).astype(jnp.bfloat16)
    xz_part = jnp.einsum(
        "xyzc,yc->xzc", features, column_weights, preferred_element_type=jnp.float32
    )
    yz_part = jnp.einsum("xyzc,xc->yzc", features, row_weights, preferred_element_type=jnp.float32)
    xy_out = plane_block(xy_plane, plane_kernels[0], rim_xy)
    xz_plane = lax.psum(xz_part, "gy").astype(jnp.bfloat16)
    xz_out = plane_block(xz_plane, plane_kernels[1], rim_xz)
    yz_plane = lax.psum(yz_part, "gx").astype(jnp.bfloat16)
    yz_out = plane_block(yz_plane, plane_kernels[2], rim_yz)
    product = xy_out.astype(jnp.float32)[:, :, None, :] * xz_out.astype(jnp.float32)[:, None, :, :]
    product = product * yz_out.astype(jnp.float32)[None, :, :, :]
    mixed = (product_scale * product).astype(jnp.bfloat16)
    hidden = jax.nn.silu(
        jnp.einsum("xyzc,ch->xyzh", mixed, expand_weight, preferred_element_type=jnp.float32)
    ).astype(jnp.bfloat16)
    branch = jnp.einsum("xyzh,hc->xyzc", hidden, shrink_weight, preferred_element_type=jnp.float32)
    return (features.astype(jnp.float32) + branch).astype(jnp.bfloat16)


def silu(v):
    half = 0.5 * v
    return half * jnp.tanh(half) + half


def taps(rows):
    n, c, w = rows.shape
    wide = rows.astype(f32).reshape(n * c, w)
    lane = lax.broadcasted_iota(jnp.int32, (n * c, w), 1)
    left = jnp.where(lane == 0, 0.0, pltpu.roll(wide, 1, 1)).astype(bf16).reshape(n, c, w)
    right = jnp.where(lane == w - 1, 0.0, pltpu.roll(wide, w - 1, 1)).astype(bf16).reshape(n, c, w)
    parts = [jnp.concatenate([left[i], rows[i], right[i]], axis=0) for i in range(n)]
    return jnp.concatenate(parts, axis=1)


def conv_rows(rows, weight):
    n, c, w = rows.shape
    full = jnp.dot(weight, taps(rows), preferred_element_type=f32)
    o = weight.shape[0] // 3
    out = []
    for i in range(n - 2):
        out.append(
            full[0:o, i * w : (i + 1) * w]
            + full[o : 2 * o, (i + 1) * w : (i + 2) * w]
            + full[2 * o : 3 * o, (i + 2) * w : (i + 3) * w]
        )
    return out


def place():
    return lax.axis_index("gx") % 4, lax.axis_index("gy")


def weighted(vox, occ, row_ref, out_ref):
    weight = jnp.broadcast_to(row_ref[...].astype(f32), vox.shape[:0:-1]).T
    occ = occ.astype(f32)
    for i in range(vox.shape[0]):
        out_ref[i] = (vox[i].astype(f32) * occ[i : i + 1] * weight).astype(out_ref.dtype)


def quarter_at(rows, chunk, d):
    low, core = place()
    quarter = rows // 8
    return pl.multiple_of(chunk_base(chunk, core, rows) + jnp.bitwise_xor(low, d) * quarter, quarter)


def fetch_kernel(row_hbm, vox_hbm, occ_hbm, column_hbm, depth_hbm, *refs):
    out_refs, more_refs, (row_ref, vox_ref, occ_ref, row_sem, vox_sem, occ_sem, more_sem) = refs[:4], refs[4:6], refs[6:]
    rows = vox_hbm.shape[0]
    quarter = rows // 8
    copies = [pltpu.make_async_copy(row_hbm, row_ref, row_sem)]
    for d in (1, 2, 3, 0):
        part = pl.ds(quarter_at(rows, 0, d), quarter)
        copies.append(pltpu.make_async_copy(vox_hbm.at[part], vox_ref.at[d], vox_sem.at[d]))
        copies.append(pltpu.make_async_copy(occ_hbm.at[part], occ_ref.at[d], occ_sem.at[d]))
    for i, source in enumerate((column_hbm, depth_hbm)):
        copies.append(pltpu.make_async_copy(source, more_refs[i], more_sem.at[i]))
    for copy in copies:
        copy.start()
    for copy in copies:
        copy.wait()
    for d in (1, 2, 3, 0):
        weighted(vox_ref[d], occ_ref[d], row_ref, out_refs[d])


def front_kernel(row_ref, vox_ref, occ_ref, after_ref, *out_refs):
    del after_ref
    rows = vox_ref.shape[0]
    for d in (1, 2, 3, 0):
        part = pl.ds(quarter_at(rows, 1, d), rows // 8)
        weighted(vox_ref[part], occ_ref[part], row_ref, out_refs[d])


def chunk_base(chunk, core, rows):
    half = rows // 2
    return (1 - core) * half if chunk == 0 else core * half


def sums_kernel(vox_ref, occ_ref, column_ref, depth_ref, after_ref, keep_ref, send_ref):
    del after_ref
    rows, c, z = vox_ref.shape
    depth = depth_ref[...].astype(f32)
    columns = column_ref[...].astype(f32).T
    at = lax.broadcasted_iota(jnp.int32, (c, z), 1) % rows
    ones = jnp.ones((2 * z, z), bf16)
    xz = jnp.zeros((c, z), f32)
    xy = jnp.zeros((c, z), f32)
    group = 8
    for base in range(0, rows, group):
        terms = []
        for y in range(base, base + group):
            feats = vox_ref[y].astype(f32) * occ_ref[y : y + 1].astype(f32)
            xz = xz + feats * columns[:, y : y + 1]
            term = feats * depth
            high = term.astype(bf16)
            terms.append(jnp.concatenate([high, (term - high.astype(f32)).astype(bf16)], axis=1))
        total = jnp.dot(jnp.concatenate(terms, axis=0), ones, preferred_element_type=f32)
        for i in range(group):
            xy = jnp.where(at == base + i, total[i * c : (i + 1) * c], xy)
    _, core = place()
    keep_ref[...] = jnp.where(core == 0, xy, xz)
    send_ref[...] = jnp.where(core == 0, xz, xy)


def merge_kernel(own_ref, first_ref, second_ref, third_ref, keep_ref, other_ref, after_ref, out_ref):
    del after_ref
    quarter, c, z = own_ref.shape
    for i in range(quarter):
        total = own_ref[i] + first_ref[i].astype(f32) + second_ref[i].astype(f32) + third_ref[i].astype(f32)
        out_ref[i] = total.astype(bf16)
    _, core = place()
    lane = lax.broadcasted_iota(jnp.int32, (c, z), 1)
    keep, other = keep_ref[...], other_ref[...]
    out_ref[quarter] = jnp.where(core == 0, jnp.where(lane < z // 2, keep, other), keep + other).astype(bf16)


def add_kernel(first_ref, second_ref, after_ref, out_ref):
    del after_ref
    out_ref[...] = (first_ref[...].astype(f32) + second_ref[...].astype(f32)).astype(bf16)


def join_kernel(sent_ref, got_ref, after_ref, first_ref, second_ref, third_ref):
    del after_ref
    quarter = sent_ref.shape[0] - 1
    for i in range(quarter):
        total = (sent_ref[i].astype(f32) + got_ref[i].astype(f32)).astype(bf16)
        for ref in (first_ref, second_ref, third_ref):
            ref[i] = total
    at = lax.axis_index("gx")
    odd = (at // 2 + at) % 2 == 1
    own, far = sent_ref[quarter], got_ref[quarter]
    first_ref[quarter] = own
    second_ref[quarter] = own
    second_ref[quarter + 1] = far
    third_ref[quarter] = jnp.where(odd, own.astype(f32), far.astype(f32)).astype(bf16)


def weights_kernel(kernel_ref, expand_ref, after_ref, small_ref, main_ref, expanded_ref):
    del after_ref
    expanded_ref[...] = expand_ref[...].astype(f32).T.astype(bf16)
    for p in range(kernel_ref.shape[0]):
        for l in range(kernel_ref.shape[1]):
            for a in range(3):
                rows = jnp.concatenate([kernel_ref[p, l, a, b] for b in range(3)], axis=0)
                o = rows.shape[1]
                value = rows.astype(f32).T.astype(bf16)
                if p < 2:
                    small_ref[p, l, a * o : (a + 1) * o] = value
                else:
                    main_ref[l, a * o : (a + 1) * o] = value


def small_kernel(*refs, last):
    near_refs, (weight_ref, edge_ref, out_ref) = refs[:5], refs[5:]
    at = lax.axis_index("gx")
    _, core = place()
    valid = [jnp.where(at > 0, 1.0, 0.0), 1.0, jnp.where(at < last, 1.0, 0.0)]
    rows = jnp.stack([ref[0] for ref in near_refs])
    inner = conv_rows(rows, weight_ref[core, 0])
    inner = jnp.stack([(silu(v) * valid[i]).astype(bf16) for i, v in enumerate(inner)])
    out_ref[0:2] = edge_ref[...]
    out_ref[2] = conv_rows(inner, weight_ref[core, 1])[0].astype(bf16)


def block(rows_ref, inner_ref, masks, first, count, operands, stage_ref, out_hbm, sem):
    vox_ref, occ_ref, own_ref, other_ref, weight_ref, expand_ref, shrink_ref = operands
    z = vox_ref.shape[2]
    inside = (count + 2) // 2
    for base in (0, inside):
        for i, v in enumerate(conv_rows(rows_ref[base : base + inside + 2], weight_ref[0])):
            v = silu(v)
            if base + i in masks:
                v = v * masks[base + i]
            inner_ref[base + i] = v.astype(bf16)
    own, far = own_ref[2].astype(f32), other_ref[2].astype(f32)
    start, other = first
    _, core = place()
    xz = jnp.where(core == 0, far, own)
    lanes = lambda plane, by: pltpu.roll(plane, z - by, 1) if by else plane
    xy = jnp.where(core == 0, lanes(own, start), lanes(far, vox_ref.shape[0] + other))
    first = jnp.where(core == 0, start, other)
    group = count // 2
    copies = []
    for base in (0, group):
        mixed = []
        for i, v in enumerate(conv_rows(inner_ref[base : base + group + 2], weight_ref[1])):
            product = xy[:, base + i : base + i + 1] * xz * v.astype(bf16).astype(f32)
            mixed.append((product_scale * product).astype(bf16))
        mixed = jnp.concatenate(mixed, axis=1)
        hidden = silu(jnp.dot(expand_ref[...], mixed, preferred_element_type=f32)).astype(bf16)
        branch = jnp.dot(shrink_ref[...], hidden, preferred_element_type=f32)
        for i in range(group):
            y = first + base + i
            feats = vox_ref[y].astype(f32) * occ_ref[pl.ds(y, 1)].astype(f32)
            stage_ref[base + i] = (feats + branch[:, i * z : (i + 1) * z]).astype(bf16)
        part = pl.ds(base, group)
        copies.append(
            pltpu.make_async_copy(stage_ref.at[part], out_hbm.at[pl.ds(first + base, group)], sem.at[base // group])
        )
        copies[-1].start()
    for copy in copies:
        copy.wait()


def near_kernel(*refs):
    pieces, operands = refs[:4], refs[4:11]
    out_hbm, edge_ref, rows_ref, inner_ref, stage_ref, sem = refs[11:]
    rows = operands[0].shape[0]
    quarter, half = rows // 8, rows // 2
    low, core = place()
    rows_ref[pl.ds(jnp.where(core == 0, half, 0), 2)] = operands[3][0:2]
    for d in range(4):
        at = jnp.where(core == 0, 0, 2) + jnp.bitwise_xor(low, d) * quarter
        rows_ref[pl.ds(at, quarter)] = pieces[d][0:quarter]
    edge_ref[...] = rows_ref[pl.ds(jnp.where(core == 0, 0, half - 2), 4)]
    block(rows_ref, inner_ref, {}, (half + 2, 0), half - 2, operands, stage_ref, out_hbm, sem)


def rest_kernel(*refs):
    pieces, edge_ref, operands = refs[:4], refs[4], refs[5:12]
    _, out_hbm, rows_ref, inner_ref, stage_ref, sem = refs[12:]
    rows, c, z = operands[0].shape
    quarter, half = rows // 8, rows // 2
    low, core = place()
    rows_ref[pl.ds(jnp.where(core == 0, 0, half + 4), 2)] = jnp.zeros((2, c, z), bf16)
    rows_ref[pl.ds(jnp.where(core == 0, half + 2, 0), 4)] = edge_ref[...]
    for d in range(4):
        at = jnp.where(core == 0, 2, 4) + jnp.bitwise_xor(low, d) * quarter
        rows_ref[pl.ds(at, quarter)] = pieces[d][...]
    masks = {0: jnp.where(core == 0, 0.0, 1.0), half + 3: jnp.where(core == 0, 1.0, 0.0)}
    block(rows_ref, inner_ref, masks, (0, half - 2), half + 2, operands, stage_ref, out_hbm, sem)


def swap(value, axis, bit):
    return lax.ppermute(value, axis, [(i, i ^ bit) for i in range(lax.axis_size(axis))])


def shifted(value, axis, by):
    size = lax.axis_size(axis)
    pairs = [(i, i - by) for i in range(size) if 0 <= i - by < size]
    return lax.ppermute(value, axis, pairs)


def vmem():
    return pl.BlockSpec(memory_space=pltpu.VMEM)


def anywhere():
    return pl.BlockSpec(memory_space=pl.ANY)


def call(kernel, name, out_shape, specs, scratch=(), mib=40):
    return pl.pallas_call(
        kernel,
        out_shape=out_shape,
        in_specs=specs,
        out_specs=jax.tree.map(lambda _: vmem(), out_shape),
        scratch_shapes=list(scratch),
        compiler_params=pltpu.CompilerParams(vmem_limit_bytes=mib * 1024 * 1024),
        name=name,
    )


def shards(
    voxels, occupancy, row_weights, column_weights, depth_weights, plane_kernels, expand_weight, shrink_weight
):
    vox = voxels.transpose(0, 1, 3, 2)[0]
    occ = occupancy[0]
    rows, c, z = vox.shape
    low, core = place()
    quarter = rows // 8
    gx_size, gx = lax.axis_size("gx"), lax.axis_index("gx")

    piece = lambda kind, n=quarter: jax.ShapeDtypeStruct((n, c, z), kind)
    shapes = [piece(f32)] + [piece(bf16)] * 3
    scratch = [
        pltpu.VMEM(row_weights.shape, bf16),
        pltpu.VMEM((4, quarter, c, z), bf16),
        pltpu.VMEM((4, quarter, z), jnp.int32),
        pltpu.SemaphoreType.DMA,
        pltpu.SemaphoreType.DMA((4,)),
        pltpu.SemaphoreType.DMA((4,)),
        pltpu.SemaphoreType.DMA((2,)),
    ]
    hbm = pl.BlockSpec(memory_space=pltpu.HBM)
    more = column_weights, depth_weights.T
    more_shapes = [jax.ShapeDtypeStruct(value.shape, bf16) for value in more]
    *first, column, depth = call(fetch_kernel, "fetch", shapes + more_shapes, [hbm] * 5, scratch, mib=62)(
        row_weights, vox, occ, *more
    )
    partners = lambda values: [swap(value, "gx", d) for d, value in zip((1, 2, 3), values)]
    first_got = partners(first[1:])
    keep, message = call(
        sums_kernel, "sums", [jax.ShapeDtypeStruct((c, z), f32)] * 2, [vmem()] * 4 + [anywhere()]
    )(vox, occ, column, depth, first_got[0])
    own, *send = call(front_kernel, "front", shapes, [vmem()] * 3 + [anywhere()])(row_weights, vox, occ, message)
    owns, gots = [first[0], own], [first_got, partners(send)]

    stacked = plane_kernels.shape[1:2] + (3 * c, 3 * c)
    small_weights, main_weights, expanded = call(
        weights_kernel,
        "weights",
        [
            jax.ShapeDtypeStruct((2,) + stacked, bf16),
            jax.ShapeDtypeStruct(stacked, bf16),
            jax.ShapeDtypeStruct(expand_weight.shape[::-1], bf16),
        ],
        [vmem()] * 2 + [anywhere()],
    )(plane_kernels, expand_weight, gots[1][0])
    merged = call(merge_kernel, "merge", piece(bf16, quarter + 1), [vmem()] * 6 + [anywhere()])(
        owns[0], *gots[0], keep, swap(message, "gy", 1), owns[1]
    )
    second = owns[1]
    for got in gots[1]:
        second = second + got.astype(f32)
    second = second.astype(bf16)
    add = lambda value, bit: (value.astype(f32) + swap(value, "gx", bit).astype(f32)).astype(bf16)
    planes = merged[quarter:]
    if gx_size == 8:
        sent = call(
            join_kernel, "join", [piece(bf16, quarter + n) for n in (1, 2, 1)], [vmem()] * 2 + [anywhere()]
        )(merged, swap(merged, "gx", 4), gots[1][2])
        got = [swap(value, "gx", d) for d, value in zip((1, 2, 3), sent)]
        second = call(add_kernel, "add", piece(bf16), [vmem()] * 2 + [anywhere()])(second, swap(second, "gx", 4), got[2])
        pieces = [[sent[0]] + got, None]
        one, two, three = (value[quarter:] for value in got)
        odd, right = gx // 2 % 2 == 1, gx % 2 == 1
        inside_only = lambda inside, value: jnp.where(inside, value, jnp.zeros_like(value))
        near = [
            inside_only(gx >= 2, jnp.where(odd, two[:1], two[1:])),
            inside_only(gx >= 1, jnp.where(right, one, three)),
            planes,
            inside_only(gx < gx_size - 1, jnp.where(right, three, one)),
            inside_only(gx < gx_size - 2, jnp.where(odd, two[1:], two[:1])),
        ]
    else:
        first, bit = merged[:quarter], 4
        while bit < gx_size:
            first, second = add(first, bit), add(second, bit)
            bit *= 2
        pieces = [[first] + [swap(first, "gx", d) for d in (1, 2, 3)], None]
        near = [shifted(planes, "gx", by) if by else planes for by in (-2, -1, 0, 1, 2)]
    pieces[1] = [second] + [swap(second, "gx", d) for d in (1, 2, 3)]
    edge = jnp.bitwise_xor(low, jnp.where(core == 0, 3, 0))
    beside = pieces[0][0][:quarter]
    for d in (1, 2, 3):
        beside = jnp.where(edge == d, pieces[0][d][:quarter], beside)
    edge = jnp.where(core == 0, beside[quarter - 2 :], beside[:2])
    small = call(
        functools.partial(small_kernel, last=gx_size - 1), "small", piece(bf16, 3), [vmem()] * 7
    )(*near, small_weights, edge)
    operands = vox, occ, small, swap(small, "gy", 1), main_weights, expanded, shrink_weight.T
    whole = jax.ShapeDtypeStruct((rows, c, z), bf16)
    half = rows // 2
    out, edge = pl.pallas_call(
        near_kernel,
        out_shape=[whole, piece(bf16, 4)],
        in_specs=[vmem()] * 11,
        out_specs=[hbm, vmem()],
        scratch_shapes=[pltpu.VMEM((n, c, z), bf16) for n in (half + 2, half, half - 2)] + [pltpu.SemaphoreType.DMA((2,))],
        compiler_params=pltpu.CompilerParams(vmem_limit_bytes=40 * 1024 * 1024),
        name="near",
    )(*pieces[0], *operands)
    out = pl.pallas_call(
        rest_kernel,
        out_shape=whole,
        in_specs=[vmem()] * 12 + [hbm],
        out_specs=hbm,
        scratch_shapes=[pltpu.VMEM((n, c, z), bf16) for n in (half + 6, half + 4, half + 2)] + [pltpu.SemaphoreType.DMA((2,))],
        input_output_aliases={12: 0},
        compiler_params=pltpu.CompilerParams(vmem_limit_bytes=40 * 1024 * 1024),
        name="rest",
    )(*pieces[1], edge, *operands, out)
    return out[None].transpose(0, 1, 3, 2)


def solution(mesh):
    in_specs = (
        P(("groups", "gx"), "gy", None, None),
        P(("groups", "gx"), "gy", None),
        P("gx", None),
        P("gy", None),
        P(),
        P(),
        P(),
        P(),
    )
    out_specs = P(("groups", "gx"), "gy", None, None)

    def whole(voxels, *rest):
        gx, gy = mesh.shape["gx"], mesh.shape["gy"]
        x, y, z = voxels.shape[0] // mesh.shape["groups"], voxels.shape[1], voxels.shape[2]
        fits = gy == 2 and gx >= 4 and gx & (gx - 1) == 0 and x == gx and y == z and z == 128
        part = shards if fits else general
        mapped = jax.shard_map(part, mesh=mesh, in_specs=in_specs, out_specs=out_specs, check_vma=False)
        return mapped(voxels, *rest)

    return whole
```

```python
import functools

import jax
import jax.numpy as jnp
from jax import lax
from jax.experimental import pallas as pl
from jax.experimental.pallas import tpu as pltpu
from jax.sharding import PartitionSpec as P

product_scale = 8.0
f32 = jnp.float32
bf16 = jnp.bfloat16


def with_halo(cells, sides, width):
    for axis, dim in sides:
        count = lax.axis_size(axis)
        ends = count - 1
        head = lax.slice_in_dim(cells, 0, width, axis=dim)
        tail = lax.slice_in_dim(cells, cells.shape[dim] - width, cells.shape[dim], axis=dim)
        cells = jnp.concatenate(
            [
                lax.ppermute(tail, axis, [(i, (i + 1) % count) for i in range(ends)]),
                cells,
                lax.ppermute(head, axis, [((i + 1) % count, i) for i in range(ends)]),
            ],
            axis=dim,
        )
    return cells


def conv_valid(padded, kernel):
    rows = padded.shape[0] - 2
    cols = padded.shape[1] - 2
    total = jnp.zeros((rows, cols, kernel.shape[-1]), jnp.float32)
    for row_off in range(3):
        for col_off in range(3):
            window = padded[row_off : row_off + rows, col_off : col_off + cols]
            total = total + jnp.einsum(
                "ijc,co->ijo", window, kernel[row_off, col_off], preferred_element_type=jnp.float32
            )
    return total


def plane_block(plane, kernels, extend):
    inner = jax.nn.silu(conv_valid(extend(plane), kernels[0])).astype(jnp.bfloat16)
    return conv_valid(extend(inner), kernels[1]).astype(jnp.bfloat16)


def rim_xy(plane):
    return with_halo(plane, (("gx", 0), ("gy", 1)), 1)


def rim_xz(plane):
    padded = with_halo(plane, (("gx", 0),), 1)
    return jnp.pad(padded, ((0, 0), (1, 1), (0, 0)))


def rim_yz(plane):
    padded = with_halo(plane, (("gy", 0),), 1)
    return jnp.pad(padded, ((0, 0), (1, 1), (0, 0)))


def general(
    voxels,
    occupancy,
    row_weights,
    column_weights,
    depth_weights,
    plane_kernels,
    expand_weight,
    shrink_weight,
):
    features = voxels * occupancy.astype(jnp.bfloat16)[..., None]
    xy_plane = jnp.einsum(
        "xyzc,zc->xyc", features, depth_weights, preferred_element_type=jnp.float32
    ).astype(jnp.bfloat16)
    xz_part = jnp.einsum(
        "xyzc,yc->xzc", features, column_weights, preferred_element_type=jnp.float32
    )
    yz_part = jnp.einsum("xyzc,xc->yzc", features, row_weights, preferred_element_type=jnp.float32)
    xy_out = plane_block(xy_plane, plane_kernels[0], rim_xy)
    xz_plane = lax.psum(xz_part, "gy").astype(jnp.bfloat16)
    xz_out = plane_block(xz_plane, plane_kernels[1], rim_xz)
    yz_plane = lax.psum(yz_part, "gx").astype(jnp.bfloat16)
    yz_out = plane_block(yz_plane, plane_kernels[2], rim_yz)
    product = xy_out.astype(jnp.float32)[:, :, None, :] * xz_out.astype(jnp.float32)[:, None, :, :]
    product = product * yz_out.astype(jnp.float32)[None, :, :, :]
    mixed = (product_scale * product).astype(jnp.bfloat16)
    hidden = jax.nn.silu(
        jnp.einsum("xyzc,ch->xyzh", mixed, expand_weight, preferred_element_type=jnp.float32)
    ).astype(jnp.bfloat16)
    branch = jnp.einsum("xyzh,hc->xyzc", hidden, shrink_weight, preferred_element_type=jnp.float32)
    return (features.astype(jnp.float32) + branch).astype(jnp.bfloat16)


def silu(v):
    half = 0.5 * v
    return half * jnp.tanh(half) + half


def taps(rows):
    n, c, w = rows.shape
    wide = rows.astype(f32).reshape(n * c, w)
    lane = lax.broadcasted_iota(jnp.int32, (n * c, w), 1)
    left = jnp.where(lane == 0, 0.0, pltpu.roll(wide, 1, 1)).astype(bf16).reshape(n, c, w)
    right = jnp.where(lane == w - 1, 0.0, pltpu.roll(wide, w - 1, 1)).astype(bf16).reshape(n, c, w)
    parts = [jnp.concatenate([left[i], rows[i], right[i]], axis=0) for i in range(n)]
    return jnp.concatenate(parts, axis=1)


def conv_rows(rows, weight):
    n, c, w = rows.shape
    full = jnp.dot(weight, taps(rows), preferred_element_type=f32)
    o = weight.shape[0] // 3
    out = []
    for i in range(n - 2):
        out.append(
            full[0:o, i * w : (i + 1) * w]
            + full[o : 2 * o, (i + 1) * w : (i + 2) * w]
            + full[2 * o : 3 * o, (i + 2) * w : (i + 3) * w]
        )
    return out


def place():
    return lax.axis_index("gx") % 4, lax.axis_index("gy")


def weighted(vox, occ, row_ref, out_ref):
    weight = jnp.broadcast_to(row_ref[...].astype(f32), vox.shape[:0:-1]).T
    occ = occ.astype(f32)
    for i in range(vox.shape[0]):
        out_ref[i] = (vox[i].astype(f32) * occ[i : i + 1] * weight).astype(out_ref.dtype)


def quarter_at(rows, chunk, d):
    low, core = place()
    quarter = rows // 8
    return pl.multiple_of(chunk_base(chunk, core, rows) + jnp.bitwise_xor(low, d) * quarter, quarter)


def fetch_kernel(row_hbm, vox_hbm, occ_hbm, column_hbm, depth_hbm, *refs):
    out_refs, more_refs, (row_ref, vox_ref, occ_ref, row_sem, vox_sem, occ_sem, more_sem) = refs[:4], refs[4:6], refs[6:]
    rows = vox_hbm.shape[0]
    quarter = rows // 8
    copies = [pltpu.make_async_copy(row_hbm, row_ref, row_sem)]
    for d in (1, 2, 3, 0):
        part = pl.ds(quarter_at(rows, 0, d), quarter)
        copies.append(pltpu.make_async_copy(vox_hbm.at[part], vox_ref.at[d], vox_sem.at[d]))
        copies.append(pltpu.make_async_copy(occ_hbm.at[part], occ_ref.at[d], occ_sem.at[d]))
    for i, source in enumerate((column_hbm, depth_hbm)):
        copies.append(pltpu.make_async_copy(source, more_refs[i], more_sem.at[i]))
    for copy in copies:
        copy.start()
    for copy in copies:
        copy.wait()
    for d in (1, 2, 3, 0):
        weighted(vox_ref[d], occ_ref[d], row_ref, out_refs[d])


def front_kernel(row_ref, vox_ref, occ_ref, after_ref, *out_refs):
    del after_ref
    rows = vox_ref.shape[0]
    for d in (1, 2, 3, 0):
        part = pl.ds(quarter_at(rows, 1, d), rows // 8)
        weighted(vox_ref[part], occ_ref[part], row_ref, out_refs[d])


def chunk_base(chunk, core, rows):
    half = rows // 2
    return (1 - core) * half if chunk == 0 else core * half


def sums_kernel(vox_ref, occ_ref, column_ref, depth_ref, after_ref, keep_ref, send_ref):
    del after_ref
    rows, c, z = vox_ref.shape
    depth = depth_ref[...].astype(f32)
    columns = column_ref[...].astype(f32).T
    at = lax.broadcasted_iota(jnp.int32, (c, z), 1) % rows
    ones = jnp.ones((2 * z, z), bf16)
    xz = jnp.zeros((c, z), f32)
    xy = jnp.zeros((c, z), f32)
    group = 8
    for base in range(0, rows, group):
        terms = []
        for y in range(base, base + group):
            feats = vox_ref[y].astype(f32) * occ_ref[y : y + 1].astype(f32)
            xz = xz + feats * columns[:, y : y + 1]
            term = feats * depth
            high = term.astype(bf16)
            terms.append(jnp.concatenate([high, (term - high.astype(f32)).astype(bf16)], axis=1))
        total = jnp.dot(jnp.concatenate(terms, axis=0), ones, preferred_element_type=f32)
        for i in range(group):
            xy = jnp.where(at == base + i, total[i * c : (i + 1) * c], xy)
    _, core = place()
    keep_ref[...] = jnp.where(core == 0, xy, xz)
    send_ref[...] = jnp.where(core == 0, xz, xy)


def merge_kernel(own_ref, first_ref, second_ref, third_ref, keep_ref, other_ref, after_ref, out_ref):
    del after_ref
    quarter, c, z = own_ref.shape
    for i in range(quarter):
        total = own_ref[i] + first_ref[i].astype(f32) + second_ref[i].astype(f32) + third_ref[i].astype(f32)
        out_ref[i] = total.astype(bf16)
    _, core = place()
    lane = lax.broadcasted_iota(jnp.int32, (c, z), 1)
    keep, other = keep_ref[...], other_ref[...]
    out_ref[quarter] = jnp.where(core == 0, jnp.where(lane < z // 2, keep, other), keep + other).astype(bf16)


def add_kernel(first_ref, second_ref, after_ref, out_ref):
    del after_ref
    out_ref[...] = (first_ref[...].astype(f32) + second_ref[...].astype(f32)).astype(bf16)


def join_kernel(sent_ref, got_ref, after_ref, first_ref, second_ref, third_ref):
    del after_ref
    quarter = sent_ref.shape[0] - 1
    for i in range(quarter):
        total = (sent_ref[i].astype(f32) + got_ref[i].astype(f32)).astype(bf16)
        for ref in (first_ref, second_ref, third_ref):
            ref[i] = total
    at = lax.axis_index("gx")
    odd = (at // 2 + at) % 2 == 1
    own, far = sent_ref[quarter], got_ref[quarter]
    first_ref[quarter] = own
    second_ref[quarter] = own
    second_ref[quarter + 1] = far
    third_ref[quarter] = jnp.where(odd, own.astype(f32), far.astype(f32)).astype(bf16)


def weights_kernel(kernel_ref, expand_ref, after_ref, small_ref, main_ref, expanded_ref):
    del after_ref
    expanded_ref[...] = expand_ref[...].astype(f32).T.astype(bf16)
    for p in range(kernel_ref.shape[0]):
        for l in range(kernel_ref.shape[1]):
            for a in range(3):
                rows = jnp.concatenate([kernel_ref[p, l, a, b] for b in range(3)], axis=0)
                o = rows.shape[1]
                value = rows.astype(f32).T.astype(bf16)
                if p < 2:
                    small_ref[p, l, a * o : (a + 1) * o] = value
                else:
                    main_ref[l, a * o : (a + 1) * o] = value


def small_kernel(*refs, last):
    near_refs, (weight_ref, edge_ref, out_ref) = refs[:5], refs[5:]
    at = lax.axis_index("gx")
    _, core = place()
    valid = [jnp.where(at > 0, 1.0, 0.0), 1.0, jnp.where(at < last, 1.0, 0.0)]
    rows = jnp.stack([ref[0] for ref in near_refs])
    inner = conv_rows(rows, weight_ref[core, 0])
    inner = jnp.stack([(silu(v) * valid[i]).astype(bf16) for i, v in enumerate(inner)])
    out_ref[0:2] = edge_ref[...]
    out_ref[2] = conv_rows(inner, weight_ref[core, 1])[0].astype(bf16)


def block(rows_ref, inner_ref, masks, first, count, operands, stage_ref, out_hbm, sem):
    vox_ref, occ_ref, own_ref, other_ref, weight_ref, expand_ref, shrink_ref = operands
    z = vox_ref.shape[2]
    inside = (count + 2) // 2
    for base in (0, inside):
        for i, v in enumerate(conv_rows(rows_ref[base : base + inside + 2], weight_ref[0])):
            v = silu(v)
            if base + i in masks:
                v = v * masks[base + i]
            inner_ref[base + i] = v.astype(bf16)
    own, far = own_ref[2].astype(f32), other_ref[2].astype(f32)
    start, other = first
    _, core = place()
    xz = jnp.where(core == 0, far, own)
    lanes = lambda plane, by: pltpu.roll(plane, z - by, 1) if by else plane
    xy = jnp.where(core == 0, lanes(own, start), lanes(far, vox_ref.shape[0] + other))
    first = jnp.where(core == 0, start, other)
    group = count // 2
    copies = []
    for base in (0, group):
        mixed = []
        for i, v in enumerate(conv_rows(inner_ref[base : base + group + 2], weight_ref[1])):
            product = xy[:, base + i : base + i + 1] * xz * v.astype(bf16).astype(f32)
            mixed.append((product_scale * product).astype(bf16))
        mixed = jnp.concatenate(mixed, axis=1)
        hidden = silu(jnp.dot(expand_ref[...], mixed, preferred_element_type=f32)).astype(bf16)
        branch = jnp.dot(shrink_ref[...], hidden, preferred_element_type=f32)
        for i in range(group):
            y = first + base + i
            feats = vox_ref[y].astype(f32) * occ_ref[pl.ds(y, 1)].astype(f32)
            stage_ref[base + i] = (feats + branch[:, i * z : (i + 1) * z]).astype(bf16)
        if out_hbm is None:
            continue
        part = pl.ds(base, group)
        copies.append(
            pltpu.make_async_copy(stage_ref.at[part], out_hbm.at[pl.ds(first + base, group)], sem.at[base // group])
        )
        copies[-1].start()
    for copy in copies:
        copy.wait()


def near_kernel(*refs):
    pieces, operands = refs[:4], refs[4:11]
    stage_ref, edge_ref, rows_ref, inner_ref = refs[11:]
    rows = operands[0].shape[0]
    quarter, half = rows // 8, rows // 2
    low, core = place()
    rows_ref[pl.ds(jnp.where(core == 0, half, 0), 2)] = operands[3][0:2]
    for d in range(4):
        at = jnp.where(core == 0, 0, 2) + jnp.bitwise_xor(low, d) * quarter
        rows_ref[pl.ds(at, quarter)] = pieces[d][0:quarter]
    edge_ref[...] = rows_ref[pl.ds(jnp.where(core == 0, 0, half - 2), 4)]
    block(rows_ref, inner_ref, {}, (half + 2, 0), half - 2, operands, stage_ref, None, None)


def rest_kernel(*refs):
    pieces, edge_ref, operands = refs[:4], refs[4], refs[5:12]
    near_ref, out_hbm, rows_ref, inner_ref, stage_ref, sem, near_sem = refs[12:]
    rows, c, z = operands[0].shape
    quarter, half = rows // 8, rows // 2
    low, core = place()
    near_rows = out_hbm.at[pl.ds(jnp.where(core == 0, half + 2, 0), half - 2)]
    near_copy = pltpu.make_async_copy(near_ref, near_rows, near_sem)
    near_copy.start()
    rows_ref[pl.ds(jnp.where(core == 0, 0, half + 4), 2)] = jnp.zeros((2, c, z), bf16)
    rows_ref[pl.ds(jnp.where(core == 0, half + 2, 0), 4)] = edge_ref[...]
    for d in range(4):
        at = jnp.where(core == 0, 2, 4) + jnp.bitwise_xor(low, d) * quarter
        rows_ref[pl.ds(at, quarter)] = pieces[d][...]
    masks = {0: jnp.where(core == 0, 0.0, 1.0), half + 3: jnp.where(core == 0, 1.0, 0.0)}
    block(rows_ref, inner_ref, masks, (0, half - 2), half + 2, operands, stage_ref, out_hbm, sem)
    near_copy.wait()


def swap(value, axis, bit):
    return lax.ppermute(value, axis, [(i, i ^ bit) for i in range(lax.axis_size(axis))])


def shifted(value, axis, by):
    size = lax.axis_size(axis)
    pairs = [(i, i - by) for i in range(size) if 0 <= i - by < size]
    return lax.ppermute(value, axis, pairs)


def vmem():
    return pl.BlockSpec(memory_space=pltpu.VMEM)


def anywhere():
    return pl.BlockSpec(memory_space=pl.ANY)


def call(kernel, name, out_shape, specs, scratch=(), mib=40):
    return pl.pallas_call(
        kernel,
        out_shape=out_shape,
        in_specs=specs,
        out_specs=jax.tree.map(lambda _: vmem(), out_shape),
        scratch_shapes=list(scratch),
        compiler_params=pltpu.CompilerParams(vmem_limit_bytes=mib * 1024 * 1024),
        name=name,
    )


def shards(
    voxels, occupancy, row_weights, column_weights, depth_weights, plane_kernels, expand_weight, shrink_weight
):
    vox = voxels.transpose(0, 1, 3, 2)[0]
    occ = occupancy[0]
    rows, c, z = vox.shape
    low, core = place()
    quarter = rows // 8
    gx_size, gx = lax.axis_size("gx"), lax.axis_index("gx")

    piece = lambda kind, n=quarter: jax.ShapeDtypeStruct((n, c, z), kind)
    shapes = [piece(f32)] + [piece(bf16)] * 3
    scratch = [
        pltpu.VMEM(row_weights.shape, bf16),
        pltpu.VMEM((4, quarter, c, z), bf16),
        pltpu.VMEM((4, quarter, z), jnp.int32),
        pltpu.SemaphoreType.DMA,
        pltpu.SemaphoreType.DMA((4,)),
        pltpu.SemaphoreType.DMA((4,)),
        pltpu.SemaphoreType.DMA((2,)),
    ]
    hbm = pl.BlockSpec(memory_space=pltpu.HBM)
    more = column_weights, depth_weights.T
    more_shapes = [jax.ShapeDtypeStruct(value.shape, bf16) for value in more]
    *first, column, depth = call(fetch_kernel, "fetch", shapes + more_shapes, [hbm] * 5, scratch, mib=62)(
        row_weights, vox, occ, *more
    )
    partners = lambda values: [swap(value, "gx", d) for d, value in zip((1, 2, 3), values)]
    first_got = partners(first[1:])
    keep, message = call(
        sums_kernel, "sums", [jax.ShapeDtypeStruct((c, z), f32)] * 2, [vmem()] * 4 + [anywhere()]
    )(vox, occ, column, depth, first_got[0])
    own, *send = call(front_kernel, "front", shapes, [vmem()] * 3 + [anywhere()])(row_weights, vox, occ, message)
    owns, gots = [first[0], own], [first_got, partners(send)]

    stacked = plane_kernels.shape[1:2] + (3 * c, 3 * c)
    small_weights, main_weights, expanded = call(
        weights_kernel,
        "weights",
        [
            jax.ShapeDtypeStruct((2,) + stacked, bf16),
            jax.ShapeDtypeStruct(stacked, bf16),
            jax.ShapeDtypeStruct(expand_weight.shape[::-1], bf16),
        ],
        [vmem()] * 2 + [anywhere()],
    )(plane_kernels, expand_weight, gots[1][0])
    merged = call(merge_kernel, "merge", piece(bf16, quarter + 1), [vmem()] * 6 + [anywhere()])(
        owns[0], *gots[0], keep, swap(message, "gy", 1), owns[1]
    )
    second = owns[1]
    for got in gots[1]:
        second = second + got.astype(f32)
    second = second.astype(bf16)
    add = lambda value, bit: (value.astype(f32) + swap(value, "gx", bit).astype(f32)).astype(bf16)
    planes = merged[quarter:]
    if gx_size == 8:
        sent = call(
            join_kernel, "join", [piece(bf16, quarter + n) for n in (1, 2, 1)], [vmem()] * 2 + [anywhere()]
        )(merged, swap(merged, "gx", 4), gots[1][2])
        got = [swap(value, "gx", d) for d, value in zip((1, 2, 3), sent)]
        second = call(add_kernel, "add", piece(bf16), [vmem()] * 2 + [anywhere()])(second, swap(second, "gx", 4), got[2])
        pieces = [[sent[0]] + got, None]
        one, two, three = (value[quarter:] for value in got)
        odd, right = gx // 2 % 2 == 1, gx % 2 == 1
        inside_only = lambda inside, value: jnp.where(inside, value, jnp.zeros_like(value))
        near = [
            inside_only(gx >= 2, jnp.where(odd, two[:1], two[1:])),
            inside_only(gx >= 1, jnp.where(right, one, three)),
            planes,
            inside_only(gx < gx_size - 1, jnp.where(right, three, one)),
            inside_only(gx < gx_size - 2, jnp.where(odd, two[1:], two[:1])),
        ]
    else:
        first, bit = merged[:quarter], 4
        while bit < gx_size:
            first, second = add(first, bit), add(second, bit)
            bit *= 2
        pieces = [[first] + [swap(first, "gx", d) for d in (1, 2, 3)], None]
        near = [shifted(planes, "gx", by) if by else planes for by in (-2, -1, 0, 1, 2)]
    pieces[1] = [second] + [swap(second, "gx", d) for d in (1, 2, 3)]
    edge = jnp.bitwise_xor(low, jnp.where(core == 0, 3, 0))
    beside = pieces[0][0][:quarter]
    for d in (1, 2, 3):
        beside = jnp.where(edge == d, pieces[0][d][:quarter], beside)
    edge = jnp.where(core == 0, beside[quarter - 2 :], beside[:2])
    small = call(
        functools.partial(small_kernel, last=gx_size - 1), "small", piece(bf16, 3), [vmem()] * 7
    )(*near, small_weights, edge)
    operands = vox, occ, small, swap(small, "gy", 1), main_weights, expanded, shrink_weight.T
    whole = jax.ShapeDtypeStruct((rows, c, z), bf16)
    half = rows // 2
    near_out, edge = pl.pallas_call(
        near_kernel,
        out_shape=[piece(bf16, half - 2), piece(bf16, 4)],
        in_specs=[vmem()] * 11,
        out_specs=[vmem(), vmem()],
        scratch_shapes=[pltpu.VMEM((n, c, z), bf16) for n in (half + 2, half)],
        compiler_params=pltpu.CompilerParams(vmem_limit_bytes=40 * 1024 * 1024),
        name="near",
    )(*pieces[0], *operands)
    out = pl.pallas_call(
        rest_kernel,
        out_shape=whole,
        in_specs=[vmem()] * 13,
        out_specs=hbm,
        scratch_shapes=[pltpu.VMEM((n, c, z), bf16) for n in (half + 6, half + 4, half + 2)]
        + [pltpu.SemaphoreType.DMA((2,)), pltpu.SemaphoreType.DMA],
        compiler_params=pltpu.CompilerParams(vmem_limit_bytes=40 * 1024 * 1024),
        name="rest",
    )(*pieces[1], edge, *operands, near_out)
    return out[None].transpose(0, 1, 3, 2)


def solution(mesh):
    in_specs = (
        P(("groups", "gx"), "gy", None, None),
        P(("groups", "gx"), "gy", None),
        P("gx", None),
        P("gy", None),
        P(),
        P(),
        P(),
        P(),
    )
    out_specs = P(("groups", "gx"), "gy", None, None)

    def whole(voxels, *rest):
        gx, gy = mesh.shape["gx"], mesh.shape["gy"]
        x, y, z = voxels.shape[0] // mesh.shape["groups"], voxels.shape[1], voxels.shape[2]
        fits = gy == 2 and gx >= 4 and gx & (gx - 1) == 0 and x == gx and y == z and z == 128
        part = shards if fits else general
        mapped = jax.shard_map(part, mesh=mesh, in_specs=in_specs, out_specs=out_specs, check_vma=False)
        return mapped(voxels, *rest)

    return whole
```
